512 devices in a mesh: dp: 8 (over y), feat: 64 (over x, z, core).
Axes of the slice: x: 4, y: 8, z: 8, core: 2. Of those that a mesh axis runs over, the one named last changes fastest.
Arguments:
- features: bfloat16 [8, 16384, 128], P('dp', None, 'feat'), may hold values from -6 to 6
- tile_weights: bfloat16 [8, 1536, 128, 128], P('dp', 'feat'), may hold values from -0.15625 to 0.15625
- tile_rows: int32 [8, 1536], P('dp', 'feat'), may hold values from 0 to 1
- tile_owners: int32 [8, 1536, 1], P('dp', 'feat'), may hold values from 0 to 63; in each aligned block of 24 rows (0 to 23, 24 to 47, ..., all dimensions but the last counted through in order) at most 2 rows name the same one
- tile_blocks: int32 [8, 1536], P('dp', 'feat'), may hold values from 0 to 1
- tile_counts: int32 [8, 64], P('dp', 'feat'), may hold values from 6 to 24, as said below
- cotangent: bfloat16 [8, 16384, 1024], P('dp', 'feat'), may hold values from -0.046875 to 0.046875
- w_self: bfloat16 [128, 1024], replicated, may hold values from -0.5 to 0.5
- w_neigh: bfloat16 [128, 1024], replicated, may hold values from -0.5 to 0.5
- bias: float32 [1024], replicated, may hold values from -4 to 4
Outputs:
- grad_self: float32 [128, 1024], P(None, 'feat')
- grad_neigh: float32 [128, 1024], P(None, 'feat')
- grad_bias: float32 [1024], P('feat')
The draws below stay inside these ranges and needn't reach their ends.
Inputs may be any that keep to these rules, and one draw needn't show every extreme that they name: `tile_owners`: among the 24 tile slots of one device at most 2 name one owner, a bound that some block of them reaches. `tile_counts`: in every batch some device has all 24 slots live.
All inputs are finite; a program needn't handle non-finite values.
Results may differ from the reference program's by a relative error of at most 0.008.
Values may be sent and summed in bfloat16 or wider, within the bound.
No kernel may reach another device: no remote copies, remote signals or barrier semaphores. Data moves between devices by JAX's collectives and lax.ppermute only.
A program may use at most 64 MiB of HBM per device.

```python
import math
import jax
import jax.numpy as jnp
import numpy as np
from jax import lax

F = 128
H = 1024
BLK = 128
NODE_DEV = 256
TILES_DEV = 24
RB_DEV = 2
NODES = 16384
BATCHES = 8
PEER_MOST = 2
N_FEAT = 64


def draw_tile_counts(key, part):
    first, second = jax.random.split(jax.random.fold_in(key, 17))
    counts = jax.random.randint(first, (BATCHES, N_FEAT), TILES_DEV // 4, TILES_DEV + 1, dtype=jnp.int32)
    fullest = jax.random.randint(second, (BATCHES, 1), 0, N_FEAT, dtype=jnp.int32)
    device_rank = jnp.arange(N_FEAT, dtype=jnp.int32)[None, :]
    return jnp.where(device_rank == fullest, TILES_DEV, counts).astype(jnp.int32)


def place_ends(entries, own_key, least, high):
    dims = entries.shape
    place = [jax.random.randint(jax.random.fold_in(own_key, axis), (), 0, dims[axis]) for axis in range(len(dims))]
    entries = entries.at[tuple(place)].set(least)
    longest = dims.index(max(dims))
    place[longest] = (place[longest] + 1) % dims[longest]
    return entries.at[tuple(place)].set(high)


def spiked(entries, own_key, source, target, shards_of, factor):
    def block_of(dim):
        return (jnp.arange(entries.shape[dim]) // (entries.shape[dim] // shards_of)).reshape((-1,) + (1,) * (entries.ndim - 1 - dim))

    near = jax.random.permutation(own_key, shards_of)[block_of(target)]
    other_side = (block_of(target) + shards_of // 2) % shards_of
    return jnp.where((block_of(source) == near) | (block_of(source) == other_side), factor * entries, entries)


def steps_of(stream_key, shape, shards, smallest, largest):
    level = 1.0
    for axis_at, blocks in shards:
        draws = jax.random.uniform(jax.random.fold_in(jax.random.fold_in(stream_key, 6), axis_at), (blocks,), jnp.float32, smallest / len(shards), largest / len(shards))
        level = level * jnp.repeat(jnp.exp(draws), shape[axis_at] // blocks).reshape((-1,) + (1,) * (len(shape) - 1 - axis_at))
    return level


def assign_block(rng, own, number, rows, number_of, top, limit, lean):
    order = jax.random.permutation(rng, number_of)
    heavy_load, common = load_shares(number_of, rows * top, limit, lean, True), load_shares(number_of, rows * top, limit, lean, False)
    places = jnp.arange(number_of)

    def named(sizes, offset_by):
        used = int((sizes > 0).sum())
        fixed = max(1, used // 4)
        passed = fixed + (places - fixed + offset_by * (used - fixed)) % max(1, number_of - fixed)
        return jnp.zeros((number_of,), jnp.int32).at[order[jnp.where(places < fixed, places, passed)]].set(jnp.asarray(sizes, jnp.int32))

    sizes = jnp.where(number % 4 == 0, named(heavy_load, number // 4), named(common, number - number // 4 - 1))
    mixed = jax.random.permutation(jax.random.fold_in(own, 3), number_of)
    donor, taker = mixed[0:number_of // 2 * 2:2], mixed[1:number_of // 2 * 2:2]
    room = jnp.minimum(sizes[donor] - 1, limit - sizes[taker]) // 2
    room = jnp.where((donor == order[0]) | (taker == order[0]) | (sizes[taker] == 0), 0, jnp.maximum(room, 0))
    passed = jax.random.randint(jax.random.fold_in(own, 4), (number_of // 2,), 0, 1 << 20) % (room + 1)
    sizes = sizes.at[donor].add(-passed).at[taker].add(passed)
    members = jnp.searchsorted(jnp.cumsum(sizes), jnp.arange(rows * top), side="right").astype(jnp.int32)
    table = members.reshape(top, rows).T
    table = table[jax.random.permutation(jax.random.fold_in(own, 1), rows)]
    offset_by = jax.random.randint(jax.random.fold_in(own, 2), (rows, 1), 0, top)
    return jnp.take_along_axis(table, (jnp.arange(top)[None, :] + offset_by) % top, axis=1)


def load_shares(count, total, reach, skew, full):
    weights = [(1 << 20) // math.isqrt(standing ** skew) + 1 for standing in range(1, count + 1)]
    largest = reach if full else min(reach, max(-(-total // count), total * weights[0] // sum(weights)))
    least = 1 if total - largest >= count - 1 else 0
    given, spare = [largest] + [least] * (count - 1), total - largest - least * (count - 1)
    while spare > 0:
        candidates = [i for i in range(1, count) if given[i] < largest] or [i for i in range(1, count) if given[i] < reach]
        whole, budget = sum([weights[i] for i in candidates]), spare
        for i in candidates:
            extra = min(reach - given[i], max(1, budget * weights[i] // whole), spare)
            given[i] = given[i] + extra
            spare = spare - extra
    return np.array(given)


def normal_values(rng, extent, deviation, most, shards=(), kind=jnp.bfloat16):
    array = jax.random.normal(rng, extent, jnp.float32) * deviation
    if len(shards) > 0:
        array = steps_of(rng, extent, shards, -0.22, 0.18) * array
    return jnp.clip(array, min=-most, max=most).astype(kind)


def gaussian_with(rng, extent, spread, most, pieces, heavy, kind=jnp.bfloat16):
    entries = spread * jax.random.normal(rng, extent, jnp.float32)
    if pieces:
        entries = entries * steps_of(rng, extent, pieces, -0.22, 0.18)
    return jnp.clip(spiked(entries, jax.random.fold_in(rng, 3), *heavy), -most, most).astype(kind)


def setup_inputs(seed: int = 0) -> dict:
    key_of = jax.random.split(jax.random.key(seed), 11)
    features = normal_values(key_of[0], (BATCHES, NODES, F), 1.0, 6.0, ((0, 8), (2, 64)))
    tile_weights = normal_values(key_of[1], (BATCHES, N_FEAT * TILES_DEV, BLK, BLK), (BLK * TILES_DEV // RB_DEV) ** -0.5, 0.15625, ((0, 8), (1, 64)))
    tile_rows = place_ends(jax.random.randint(key_of[2], (BATCHES, N_FEAT * TILES_DEV), 0, RB_DEV), jax.random.fold_in(key_of[2], 1), 0, RB_DEV - 1).astype(jnp.int32)
    tile_owners_keys = jax.random.split(jax.random.fold_in(key_of[3], 1), BATCHES * (N_FEAT * TILES_DEV) // TILES_DEV)
    tile_owners_turns = jax.random.permutation(jax.random.fold_in(key_of[3], 3), BATCHES * (N_FEAT * TILES_DEV) // TILES_DEV)
    tile_owners = jax.vmap(lambda own, number: assign_block(jax.random.fold_in(key_of[3], 2), own, number, TILES_DEV, N_FEAT, 1, PEER_MOST, 2))(tile_owners_keys, tile_owners_turns).reshape((BATCHES, N_FEAT * TILES_DEV, 1))
    tile_blocks = place_ends(jax.random.randint(key_of[4], (BATCHES, N_FEAT * TILES_DEV), 0, RB_DEV), jax.random.fold_in(key_of[4], 1), 0, RB_DEV - 1).astype(jnp.int32)
    tile_counts = draw_tile_counts(jax.random.fold_in(key_of[10], 71), 0)
    cotangent = gaussian_with(key_of[6], (BATCHES, NODES, H), (1.0 / (BATCHES * NODES) ** 0.5), 0.046875, ((0, 8), (1, 64)), (1, 2, 64, 4.0))
    w_self = normal_values(key_of[7], (F, H), F ** -0.5, 0.5)
    w_neigh = normal_values(key_of[8], (F, H), F ** -0.5, 0.5)
    bias = normal_values(key_of[9], (H,), 1.0, 4.0, (), jnp.float32)
    return dict(features=features, tile_weights=tile_weights, tile_rows=tile_rows, tile_owners=tile_owners, tile_blocks=tile_blocks, tile_counts=tile_counts, cotangent=cotangent, w_self=w_self, w_neigh=w_neigh, bias=bias)


def silu_slope(pre_act):
    sigmoid_z = jax.nn.sigmoid(pre_act)
    return sigmoid_z * (1.0 + pre_act * (1.0 - sigmoid_z))


def reference(features, tile_weights, tile_rows, tile_owners, tile_blocks, tile_counts, cotangent, w_self, w_neigh, bias):
    block_total = NODES // BLK

    def accumulate(carry, member):
        batch = member // N_FEAT
        device = member % N_FEAT
        feats = lax.dynamic_index_in_dim(features, batch, 0, keepdims=False)
        base = (device * TILES_DEV).astype(jnp.int32)
        tiles = lax.dynamic_slice_in_dim(lax.dynamic_index_in_dim(tile_weights, batch, 0, keepdims=False), base, TILES_DEV, 0)
        rows_here = lax.dynamic_slice_in_dim(lax.dynamic_index_in_dim(tile_rows, batch, 0, keepdims=False), base, TILES_DEV, 0)
        owners_here = lax.dynamic_slice_in_dim(lax.dynamic_index_in_dim(tile_owners, batch, 0, keepdims=False)[:, 0], base, TILES_DEV, 0)
        blocks_here = lax.dynamic_slice_in_dim(lax.dynamic_index_in_dim(tile_blocks, batch, 0, keepdims=False), base, TILES_DEV, 0)
        count = lax.dynamic_index_in_dim(lax.dynamic_index_in_dim(tile_counts, batch, 0, keepdims=False), device, 0, keepdims=False)
        picked = feats.reshape(block_total, BLK, F)[owners_here * RB_DEV + blocks_here]
        products = jnp.einsum("kij,kjf->kif", tiles.astype(jnp.float32), picked.astype(jnp.float32), precision=lax.Precision.HIGHEST)
        live = jnp.arange(TILES_DEV, dtype=jnp.int32) < count
        select = ((rows_here[None, :] == jnp.arange(RB_DEV, dtype=jnp.int32)[:, None]) & live[None, :]).astype(jnp.float32)
        summed = jnp.einsum("rk,kif->rif", select, products, precision=lax.Precision.HIGHEST)
        neighbour = summed.reshape(NODE_DEV, F).astype(jnp.bfloat16)
        start = (device * NODE_DEV).astype(jnp.int32)
        owned = lax.dynamic_slice_in_dim(feats, start, NODE_DEV, 0)
        upstream = lax.dynamic_slice_in_dim(lax.dynamic_index_in_dim(cotangent, batch, 0, keepdims=False), start, NODE_DEV, 0)
        pre_act = jnp.dot(owned, w_self, preferred_element_type=jnp.float32) + jnp.dot(neighbour, w_neigh, preferred_element_type=jnp.float32) + bias
        slope = (upstream.astype(jnp.float32) * silu_slope(pre_act)).astype(jnp.bfloat16)
        grad_s = jnp.dot(owned.T, slope, preferred_element_type=jnp.float32)
        grad_n = jnp.dot(neighbour.T, slope, preferred_element_type=jnp.float32)
        grad_b = jnp.sum(slope.astype(jnp.float32), axis=0)
        return (carry[0] + grad_s, carry[1] + grad_n, carry[2] + grad_b), None

    start_sums = (jnp.zeros((F, H), jnp.float32), jnp.zeros((F, H), jnp.float32), jnp.zeros((H,), jnp.float32))
    totals, _ = lax.scan(accumulate, start_sums, jnp.arange(BATCHES * N_FEAT, dtype=jnp.int32))
    return (totals[0], totals[1], totals[2])
```

```python
import jax
import jax.numpy as jnp
from jax import lax
from jax.experimental import pallas as pl
from jax.experimental.pallas import tpu as pltpu
from jax.sharding import Mesh, PartitionSpec as P

CORES = 2
LANES = 128
PAD_SLOTS = 32
BF16, F32 = jnp.bfloat16, jnp.float32
VMEM = pl.BlockSpec(memory_space=pltpu.VMEM)
SMEM = pl.BlockSpec(memory_space=pltpu.SMEM)
LIMIT = 56 * 1024 * 1024


def call(kernel, outs, specs, scratch=(), cost=None):
    return pl.pallas_call(
        kernel,
        out_shape=outs,
        in_specs=specs,
        out_specs=jax.tree.map(lambda _: VMEM, outs),
        scratch_shapes=list(scratch),
        compiler_params=pltpu.CompilerParams(vmem_limit_bytes=LIMIT),
        cost_estimate=cost,
    )


def pack_kernel(core_ref, lists_ref, own_ref, other_ref, sent_ref, pairs_ref):
    blocks = own_ref.shape[1] // LANES
    width = own_ref.shape[0]
    core = core_ref[0]
    for side, ref in enumerate((own_ref, other_ref)):
        place = side + core - 2 * side * core
        for b in range(blocks):
            pairs_ref[place, pl.ds(width * b, width), :] = ref[
                :, b * LANES : (b + 1) * LANES
            ].astype(F32)
    table = jnp.concatenate(
        [
            pairs_ref[c, pl.ds(f, blocks, stride=width), :].astype(BF16)
            for c in range(CORES)
            for f in range(width)
        ],
        axis=1,
    )
    group = LANES // PAD_SLOTS
    lane_group = lax.broadcasted_iota(jnp.int32, (1, LANES), 1) // PAD_SLOTS
    block_of = lax.broadcasted_iota(jnp.int32, (blocks, LANES), 0)
    for g in range(lists_ref.shape[0] // group):
        row = lists_ref[g * group]
        for j in range(1, group):
            row = jnp.where(lane_group == j, lists_ref[g * group + j], row)
        chosen = jnp.where(block_of == row, 1.0, 0.0).astype(BF16)
        sent_ref[g * LANES : (g + 1) * LANES, :] = lax.dot_general(
            chosen, table, (((0,), (0,)), ((), ())), preferred_element_type=F32
        ).astype(BF16)


def layer_kernel(
    core_ref,
    count_ref,
    rows_ref,
    got_ref,
    tiles_ref,
    cot_ref,
    w_self_ref,
    w_neigh_ref,
    bias_ref,
    kept_ref,
    away_ref,
    wide_ref,
    picked_ref,
    masked_ref,
    order_ref,
    grad_ref,
):
    columns = wide_ref.shape[0]
    slots, side = tiles_ref.shape[0], tiles_ref.shape[1]
    chips = got_ref.shape[0] // PAD_SLOTS
    feats = columns * chips
    for q in range(columns):
        wide_ref[q] = got_ref[:, q * LANES : (q + 1) * LANES].astype(F32)

    def block(slot):
        return jnp.concatenate(
            [wide_ref[q, pl.ds(slot, chips, stride=PAD_SLOTS), :] for q in range(columns)],
            axis=0,
        )

    row_blocks = masked_ref.shape[0] // side
    for s in range(slots):
        at = slice(s * side, (s + 1) * side)
        picked_ref[:, at] = block(s).astype(BF16)
        tile = tiles_ref[s]
        live = s < count_ref[0]
        for r in range(row_blocks):
            use = jnp.logical_and(live, rows_ref[s] == r)
            masked_ref[r * side : (r + 1) * side, at] = jnp.where(
                use, tile, jnp.zeros_like(tile)
            )
    agg = lax.dot_general(
        picked_ref[...],
        masked_ref[...],
        (((1,), (1,)), ((), ())),
        preferred_element_type=F32,
    )

    def node_major(r, value):
        for q in range(columns):
            order_ref[r, pl.ds(q, chips, stride=columns), :] = value[
                q * chips : (q + 1) * chips
            ]
        return order_ref[r].T.astype(BF16)

    nodes = []
    for r in range(row_blocks):
        nodes.append(
            jnp.concatenate(
                [
                    node_major(2 * r, block(slots + r)),
                    node_major(2 * r + 1, agg[:, r * side : (r + 1) * side]),
                ],
                axis=1,
            )
        )
    inputs = jnp.concatenate(nodes, axis=0)
    weights = jnp.concatenate([w_self_ref[...], w_neigh_ref[...]], axis=0)
    pre = jnp.dot(inputs, weights, preferred_element_type=F32) + bias_ref[...]
    s = jax.nn.sigmoid(pre)
    slope = (cot_ref[...].astype(F32) * (s * (1.0 + pre * (1.0 - s)))).astype(BF16)
    ones = jnp.ones((inputs.shape[0], LANES), BF16)
    grad_ref[...] = lax.dot_general(
        slope,
        jnp.concatenate([inputs, ones], axis=1),
        (((0,), (0,)), ((), ())),
        preferred_element_type=F32,
    )
    part = kept_ref.shape[0] // chips
    core = core_ref[0]
    for k in range(chips):
        at = slice(k * part, (k + 1) * part)
        here = pl.multiple_of(k * CORES * part + core * part, part)
        there = pl.multiple_of(k * CORES * part + (1 - core) * part, part)
        kept_ref[at, :] = grad_ref[pl.ds(here, part), :]
        away_ref[at, :] = grad_ref[pl.ds(there, part), :].astype(BF16)


def add_kernel(kept_ref, came_ref, out_ref):
    out_ref[...] = (kept_ref[...] + came_ref[...].astype(F32)).astype(BF16)


def spread_kernel(got_ref, out_ref):
    total = jnp.sum(got_ref[...].astype(F32), axis=0)
    for b in range(out_ref.shape[0]):
        out_ref[b] = total


def final_kernel(got_ref, self_ref, neigh_ref, bias_ref):
    total = jnp.sum(got_ref[...], axis=0)
    feats = self_ref.shape[1]
    self_ref[...] = total[:, :feats]
    neigh_ref[...] = total[:, feats : 2 * feats]
    bias_ref[...] = total[:, 2 * feats : 3 * feats].T[:1]


def local(
    features,
    tile_weights,
    tile_rows,
    tile_owners,
    tile_blocks,
    tile_counts,
    cotangent,
    w_self,
    w_neigh,
    bias,
):
    own = features[0].T
    width, node_count = own.shape
    slots, side = tile_weights.shape[1], tile_weights.shape[2]
    chips = lax.axis_size("chip")
    batches = lax.axis_size("dp")
    feats, hidden = w_self.shape
    nodes_here = cotangent.shape[1]
    row_blocks = nodes_here // side
    core = lax.axis_index("core")
    device = lax.axis_index("chip") * CORES + core
    swap = [(i, CORES - 1 - i) for i in range(CORES)]

    other = lax.ppermute(own, "core", swap)
    named = tile_owners[0, :, 0] * row_blocks + tile_blocks[0]
    mine = device * row_blocks + jnp.arange(row_blocks, dtype=jnp.int32)
    rest = jnp.zeros((PAD_SLOTS - slots - row_blocks,), jnp.int32)
    names = jnp.concatenate([named, mine, rest])
    names = jnp.broadcast_to(
        jnp.tile(names, LANES // PAD_SLOTS)[None, None], (chips, 1, LANES)
    )
    lists = lax.all_to_all(names, "chip", split_axis=0, concat_axis=0, tiled=True)

    core_at = core[None].astype(jnp.int32)
    columns = CORES * width
    sent = call(
        pack_kernel,
        jax.ShapeDtypeStruct((chips * PAD_SLOTS, columns * side), BF16),
        [SMEM, VMEM, VMEM, VMEM],
        [pltpu.VMEM((CORES, node_count // side * width, side), F32)],
    )(core_at, lists, own, other)
    got = lax.all_to_all(
        sent.reshape(chips, PAD_SLOTS, columns * side),
        "chip",
        split_axis=0,
        concat_axis=0,
        tiled=True,
    ).reshape(chips * PAD_SLOTS, columns * side)

    part = hidden // (chips * CORES)
    wide = 2 * feats + LANES
    kept, away = call(
        layer_kernel,
        (
            jax.ShapeDtypeStruct((chips * part, wide), F32),
            jax.ShapeDtypeStruct((chips * part, wide), BF16),
        ),
        [SMEM, SMEM, SMEM] + [VMEM] * 6,
        [
            pltpu.VMEM((columns, chips * PAD_SLOTS, side), F32),
            pltpu.VMEM((feats, slots * side), BF16),
            pltpu.VMEM((row_blocks * side, slots * side), BF16),
            pltpu.VMEM((2 * row_blocks, feats, side), F32),
            pltpu.VMEM((hidden, wide), F32),
        ],
    )(
        core_at,
        tile_counts[0],
        tile_rows[0],
        got,
        tile_weights[0],
        cotangent[0],
        w_self,
        w_neigh,
        bias[None],
    )
    came = lax.ppermute(away, "core", swap)
    summed = call(
        add_kernel,
        jax.ShapeDtypeStruct(away.shape, BF16),
        [VMEM, VMEM],
    )(kept, came).reshape(chips, part, wide)
    parts = lax.all_to_all(summed, "chip", split_axis=0, concat_axis=0, tiled=True)
    spread = call(
        spread_kernel, jax.ShapeDtypeStruct((batches, part, wide), F32), [VMEM]
    )(parts)
    totals = lax.all_to_all(spread, "dp", split_axis=0, concat_axis=0, tiled=True)
    out_s, out_n, out_b = call(
        final_kernel,
        (
            jax.ShapeDtypeStruct((part, feats), F32),
            jax.ShapeDtypeStruct((part, feats), F32),
            jax.ShapeDtypeStruct((1, part), F32),
        ),
        [VMEM],
    )(totals)
    return (out_s.T, out_n.T, out_b[0])


def solution(mesh):
    batches, owners = mesh.devices.shape
    split = Mesh(
        mesh.devices.reshape(batches, owners // CORES, CORES), ("dp", "chip", "core")
    )
    feat = ("chip", "core")
    return jax.shard_map(
        local,
        mesh=split,
        in_specs=(
            P("dp", None, feat),
            P("dp", feat, None, None),
            P("dp", feat),
            P("dp", feat, None),
            P("dp", feat),
            P("dp", feat),
            P("dp", feat, None),
            P(),
            P(),
            P(),
        ),
        out_specs=(P(None, feat), P(None, feat), P(feat)),
        check_vma=False,
    )
```

```python
import functools

import jax
import jax.numpy as jnp
from jax import lax
from jax.experimental import pallas as pl
from jax.experimental.pallas import tpu as pltpu
from jax.sharding import Mesh, PartitionSpec as P

CORES, DEPTH = 2, 8
LANES, SUBLANES = 128, 8
BF16, F32 = jnp.bfloat16, jnp.float32
VMEM = pl.BlockSpec(memory_space=pltpu.VMEM)
SMEM = pl.BlockSpec(memory_space=pltpu.SMEM)
MIB = 1024 * 1024
FIRST = (((0,), (0,)), ((), ()))
LAST = (((1,), (1,)), ((), ()))


def call(kernel, outs, specs, mib, scratch=()):
    return pl.pallas_call(
        kernel,
        out_shape=outs,
        in_specs=specs,
        out_specs=jax.tree.map(lambda _: VMEM, outs),
        scratch_shapes=list(scratch),
        compiler_params=pltpu.CompilerParams(vmem_limit_bytes=mib * MIB),
    )


def pack_kernel(lists_ref, whole_ref, sent_ref):
    depth, width = whole_ref.shape[0], whole_ref.shape[1]
    slots = sent_ref.shape[2] // LANES

    def peer(p, carry):
        for s in range(slots):
            at = pl.ds(pl.multiple_of(lists_ref[p, 0, s] * LANES, LANES), LANES)
            here = slice(s * LANES, (s + 1) * LANES)
            for z in range(depth):
                sent_ref[p, z * width : (z + 1) * width, here] = whole_ref[z, :, at]
        return carry

    lax.fori_loop(0, sent_ref.shape[0], peer, 0)


def gather_kernel(width, count_ref, rows_ref, got_ref, tiles_ref, inputs_ref, masked_ref):
    slots, side = tiles_ref.shape[0], tiles_ref.shape[1]
    feats = got_ref.shape[0]
    row_blocks = masked_ref.shape[0] // side
    for s in range(slots):
        tile = tiles_ref[s]
        live = s < count_ref[0]
        here = slice(s * side, (s + 1) * side)
        for r in range(row_blocks):
            use = jnp.logical_and(live, rows_ref[s] == r)
            masked_ref[r * side : (r + 1) * side, here] = jnp.where(
                use, tile, jnp.zeros_like(tile)
            )
    agg = lax.dot_general(
        got_ref[:, : slots * side],
        masked_ref[...],
        LAST,
        preferred_element_type=F32,
    ).astype(BF16)
    row = lax.broadcasted_iota(jnp.int32, (feats, feats), 0)
    feature = lax.broadcasted_iota(jnp.int32, (feats, feats), 1)
    column = row % width
    z = row // width % DEPTH
    core = row // (width * DEPTH) % CORES
    x = row // (width * DEPTH * CORES)
    place = ((x * DEPTH + z) * CORES + core) * width + column
    order = jnp.where(place == feature, 1.0, 0.0).astype(BF16)
    for k, value in enumerate((got_ref[:, slots * side :], agg)):
        inputs_ref[:, k * feats : (k + 1) * feats] = lax.dot_general(
            value, order, FIRST, preferred_element_type=F32
        ).astype(BF16)


def split_kernel(
    part,
    core_ref,
    cot_ref,
    w_self_ref,
    w_neigh_ref,
    bias_ref,
    mine_ref,
    theirs_ref,
    weights_ref,
    half_bias_ref,
):
    pair = CORES * LANES
    lane = lax.broadcasted_iota(jnp.int32, (pair, LANES), 0)
    to = lax.broadcasted_iota(jnp.int32, (pair, LANES), 1)
    group = to // part * (CORES * part) + to % part
    here = jnp.where(lane == group + core_ref[0] * part, 1.0, 0.0)
    there = jnp.where(lane == group + (1 - core_ref[0]) * part, 1.0, 0.0)
    here16, there16 = here.astype(BF16), there.astype(BF16)
    feats = w_self_ref.shape[0]

    def pick(value, chosen):
        return jnp.dot(value, chosen, preferred_element_type=F32).astype(BF16)

    for m in range(mine_ref.shape[1] // LANES):
        out = slice(m * LANES, (m + 1) * LANES)
        wide = slice(m * pair, (m + 1) * pair)
        mine_ref[:, out] = pick(cot_ref[:, wide], here16)
        theirs_ref[:, out] = pick(cot_ref[:, wide], there16)
        weights_ref[:feats, out] = pick(w_self_ref[:, wide], here16)
        weights_ref[feats:, out] = pick(w_neigh_ref[:, wide], here16)
        half_bias_ref[:, out] = jnp.dot(
            jnp.broadcast_to(bias_ref[:, wide], (SUBLANES, pair)),
            here,
            precision=lax.Precision.HIGHEST,
            preferred_element_type=F32,
        )[:1]


def layer_kernel(
    mine_ref, theirs_ref, cot_ref, their_cot_ref, weights_ref, bias_ref, sent_ref
):
    half = cot_ref.shape[1]
    weights, bias = weights_ref[...], bias_ref[...]
    total, sums = 0.0, 0.0
    for inputs, cot in (
        (mine_ref[...], cot_ref[...]),
        (theirs_ref[...], their_cot_ref[...]),
    ):
        pre = jnp.dot(inputs, weights, preferred_element_type=F32) + bias
        s = jax.nn.sigmoid(pre)
        slope = (cot.astype(F32) * (s * (1.0 + pre * (1.0 - s)))).astype(BF16)
        total += lax.dot_general(slope, inputs, FIRST, preferred_element_type=F32)
        sums += jnp.sum(slope.astype(F32), axis=0, keepdims=True)
    chips, rows = sent_ref.shape[0], sent_ref.shape[1]
    part = half // chips
    feats = total.shape[1] // 2
    total = total.astype(BF16)
    tail = jnp.concatenate(
        [sums[:, k * LANES : (k + 1) * LANES] for k in range(half // LANES)]
        + [jnp.zeros((SUBLANES - half // LANES, LANES), F32)],
        axis=0,
    ).astype(BF16)
    for k in range(chips):
        here = slice(k * part, (k + 1) * part)
        sent_ref[k, :part, :] = total[here, :feats]
        sent_ref[k, part : 2 * part, :] = total[here, feats:]
        sent_ref[k, 2 * part : rows, :] = tail


def spread_kernel(got_ref, out_ref):
    total = jnp.sum(got_ref[...].astype(F32), axis=0)
    for b in range(out_ref.shape[0]):
        out_ref[b] = total


def final_kernel(chip_ref, got_ref, self_ref, neigh_ref, bias_ref, sums_ref):
    part = self_ref.shape[0]
    total = jnp.sum(got_ref[...], axis=0)
    self_ref[...] = total[:part]
    neigh_ref[...] = total[part : 2 * part]
    sums_ref[...] = total[2 * part :]
    per_row = LANES // part
    row = sums_ref[pl.ds(chip_ref[0] // per_row, 1), :]
    lane = lax.broadcasted_iota(jnp.int32, (LANES, LANES), 0)
    to = lax.broadcasted_iota(jnp.int32, (LANES, LANES), 1)
    shift = chip_ref[0] % per_row * part
    moved = jnp.where(lane == to + shift, jnp.broadcast_to(row, (LANES, LANES)).T, 0.0)
    bias_ref[...] = jnp.sum(moved, axis=0, keepdims=True)[:, :part]


def local(
    features,
    tile_weights,
    tile_rows,
    tile_owners,
    tile_blocks,
    tile_counts,
    cotangent,
    w_self,
    w_neigh,
    bias,
):
    own = features[0].T
    width, node_count = own.shape
    slots, side = tile_weights.shape[1], tile_weights.shape[2]
    batches = lax.axis_size("dp")
    peers = lax.axis_size("x") * CORES
    chips = lax.axis_size("x") * DEPTH
    feats, hidden = w_self.shape
    nodes_here = cotangent.shape[1]
    row_blocks = nodes_here // side
    core = lax.axis_index("core")
    chip = lax.axis_index("x") * DEPTH + lax.axis_index("z")
    core_at, chip_at = core[None], chip[None]
    swap = [(i, CORES - 1 - i) for i in range(CORES)]

    whole = lax.all_to_all(
        jnp.broadcast_to(own[None], (DEPTH, width, node_count)),
        "z",
        split_axis=0,
        concat_axis=0,
        tiled=True,
    )
    half = hidden // CORES
    part = half // chips
    cot, away, weights, half_bias = call(
        functools.partial(split_kernel, part),
        (
            jax.ShapeDtypeStruct((nodes_here, half), BF16),
            jax.ShapeDtypeStruct((nodes_here, half), BF16),
            jax.ShapeDtypeStruct((2 * feats, half), BF16),
            jax.ShapeDtypeStruct((1, half), F32),
        ),
        [SMEM] + [VMEM] * 4,
        12,
    )(core_at, cotangent[0], w_self, w_neigh, bias[None])
    their_cot = lax.ppermute(away, "core", swap)
    named = tile_owners[0, :, 0] * row_blocks + tile_blocks[0]
    held = (chip * CORES + core) * row_blocks + jnp.arange(row_blocks, dtype=jnp.int32)
    names = jnp.pad(jnp.concatenate([named, held]), (0, LANES - slots - row_blocks))
    lists = lax.all_to_all(
        jnp.broadcast_to(names[None, None], (peers, 1, LANES)),
        ("x", "core"),
        split_axis=0,
        concat_axis=0,
        tiled=True,
    )
    sent = call(
        pack_kernel,
        jax.ShapeDtypeStruct((peers, DEPTH * width, (slots + row_blocks) * side), BF16),
        [SMEM, VMEM],
        8,
    )(lists, whole)
    got = lax.all_to_all(
        sent, ("x", "core"), split_axis=0, concat_axis=0, tiled=True
    ).reshape(feats, (slots + row_blocks) * side)
    mine = call(
        functools.partial(gather_kernel, width),
        jax.ShapeDtypeStruct((nodes_here, 2 * feats), BF16),
        [SMEM, SMEM, VMEM, VMEM],
        12,
        [pltpu.VMEM((row_blocks * side, slots * side), BF16)],
    )(tile_counts[0], tile_rows[0], got, tile_weights[0])
    theirs = lax.ppermute(mine, "core", swap)
    rows = 2 * part + SUBLANES
    sums = call(
        layer_kernel,
        jax.ShapeDtypeStruct((chips, rows, feats), BF16),
        [VMEM] * 6,
        16,
    )(mine, theirs, cot, their_cot, weights, half_bias)
    parts = lax.all_to_all(sums, ("x", "z"), split_axis=0, concat_axis=0, tiled=True)
    spread = call(
        spread_kernel,
        jax.ShapeDtypeStruct((batches, rows, feats), F32),
        [VMEM],
        4,
    )(parts)
    totals = lax.all_to_all(spread, "dp", split_axis=0, concat_axis=0, tiled=True)
    out_s, out_n, out_b = call(
        final_kernel,
        (
            jax.ShapeDtypeStruct((part, feats), F32),
            jax.ShapeDtypeStruct((part, feats), F32),
            jax.ShapeDtypeStruct((1, part), F32),
        ),
        [SMEM, VMEM],
        4,
        [pltpu.VMEM((SUBLANES, LANES), F32)],
    )(chip_at, totals)
    return (out_s.T, out_n.T, out_b[0])


def solution(mesh):
    batches, owners = mesh.devices.shape
    split = Mesh(
        mesh.devices.reshape(batches, owners // (DEPTH * CORES), DEPTH, CORES),
        ("dp", "x", "z", "core"),
    )
    feat = ("x", "z", "core")
    return jax.shard_map(
        local,
        mesh=split,
        in_specs=(
            P("dp", None, feat),
            P("dp", feat, None, None),
            P("dp", feat),
            P("dp", feat, None),
            P("dp", feat),
            P("dp", feat),
            P("dp", feat, None),
            P(),
            P(),
            P(),
        ),
        out_specs=(P(None, feat), P(None, feat), P(feat)),
        check_vma=False,
    )
```

```python
import functools

import jax
import jax.numpy as jnp
from jax import lax
from jax.experimental import pallas as pl
from jax.experimental.pallas import tpu as pltpu
from jax.sharding import Mesh, PartitionSpec as P

CORES, DEPTH = 2, 8
LANES, SUBLANES = 128, 8
BF16, F32 = jnp.bfloat16, jnp.float32
VMEM = pl.BlockSpec(memory_space=pltpu.VMEM)
SMEM = pl.BlockSpec(memory_space=pltpu.SMEM)
MIB = 1024 * 1024
FIRST = (((0,), (0,)), ((), ()))
LAST = (((1,), (1,)), ((), ()))


def call(kernel, outs, specs, mib, scratch=()):
    return pl.pallas_call(
        kernel,
        out_shape=outs,
        in_specs=specs,
        out_specs=jax.tree.map(lambda _: VMEM, outs),
        scratch_shapes=list(scratch),
        compiler_params=pltpu.CompilerParams(vmem_limit_bytes=mib * MIB),
    )


def pack_kernel(at_ref, *refs):
    *lists_refs, whole_ref, sent_ref = refs
    depth, width = whole_ref.shape[0], whole_ref.shape[1]
    slots = sent_ref.shape[2] // LANES
    reach = len(lists_refs)
    for step, lists_ref in enumerate(lists_refs):
        x = lax.rem(at_ref[0] + reach - step, reach)

        def peer(side, carry, x=x, lists_ref=lists_ref):
            p = x * CORES + lax.rem(at_ref[1] + side, CORES)
            for s in range(slots):
                at = pl.ds(pl.multiple_of(lists_ref[side, s] * LANES, LANES), LANES)
                here = slice(s * LANES, (s + 1) * LANES)
                for z in range(depth):
                    sent_ref[p, z * width : (z + 1) * width, here] = whole_ref[z, :, at]
            return carry

        lax.fori_loop(0, CORES, peer, 0)


def gather_kernel(width, got_ref, masked_ref, inputs_ref):
    feats = got_ref.shape[0]
    named = masked_ref.shape[1]
    agg = lax.dot_general(
        got_ref[:, :named],
        masked_ref[...],
        LAST,
        preferred_element_type=F32,
    ).astype(BF16)
    row = lax.broadcasted_iota(jnp.int32, (feats, feats), 0)
    feature = lax.broadcasted_iota(jnp.int32, (feats, feats), 1)
    column = row % width
    z = row // width % DEPTH
    core = row // (width * DEPTH) % CORES
    x = row // (width * DEPTH * CORES)
    place = ((x * DEPTH + z) * CORES + core) * width + column
    order = jnp.where(place == feature, 1.0, 0.0).astype(BF16)
    for k, value in enumerate((got_ref[:, named:], agg)):
        inputs_ref[:, k * feats : (k + 1) * feats] = lax.dot_general(
            value, order, FIRST, preferred_element_type=F32
        ).astype(BF16)


def split_kernel(
    part,
    core_ref,
    cot_ref,
    w_self_ref,
    w_neigh_ref,
    bias_ref,
    rows_ref,
    tiles_ref,
    mine_ref,
    theirs_ref,
    weights_ref,
    half_bias_ref,
    masked_ref,
):
    slots, side = tiles_ref.shape[0], tiles_ref.shape[1]
    for s in range(slots):
        tile = tiles_ref[s]
        for r in range(masked_ref.shape[0] // side):
            masked_ref[r * side : (r + 1) * side, s * side : (s + 1) * side] = jnp.where(
                rows_ref[s] == r, tile, jnp.zeros_like(tile)
            )
    pair = CORES * LANES
    lane = lax.broadcasted_iota(jnp.int32, (pair, LANES), 0)
    to = lax.broadcasted_iota(jnp.int32, (pair, LANES), 1)
    group = to // part * (CORES * part) + to % part
    here = jnp.where(lane == group + core_ref[0] * part, 1.0, 0.0)
    there = jnp.where(lane == group + (1 - core_ref[0]) * part, 1.0, 0.0)
    here16, there16 = here.astype(BF16), there.astype(BF16)
    feats = w_self_ref.shape[0]

    def pick(value, chosen):
        return jnp.dot(value, chosen, preferred_element_type=F32).astype(BF16)

    for m in range(mine_ref.shape[1] // LANES):
        out = slice(m * LANES, (m + 1) * LANES)
        wide = slice(m * pair, (m + 1) * pair)
        mine_ref[:, out] = pick(cot_ref[:, wide], here16)
        theirs_ref[:, out] = pick(cot_ref[:, wide], there16)
        weights_ref[:feats, out] = pick(w_self_ref[:, wide], here16)
        weights_ref[feats:, out] = pick(w_neigh_ref[:, wide], here16)
        half_bias_ref[:, out] = jnp.dot(
            jnp.broadcast_to(bias_ref[:, wide], (SUBLANES, pair)),
            here,
            precision=lax.Precision.HIGHEST,
            preferred_element_type=F32,
        )[:1]


def layer_kernel(
    mine_ref, theirs_ref, cot_ref, their_cot_ref, weights_ref, bias_ref, sent_ref
):
    half = cot_ref.shape[1]
    weights, bias = weights_ref[...], bias_ref[...]
    total, sums = 0.0, 0.0
    for inputs, cot in (
        (mine_ref[...], cot_ref[...]),
        (theirs_ref[...], their_cot_ref[...]),
    ):
        pre = jnp.dot(inputs, weights, preferred_element_type=F32) + bias
        s = jax.nn.sigmoid(pre)
        slope = (cot.astype(F32) * (s * (1.0 + pre * (1.0 - s)))).astype(BF16)
        total += lax.dot_general(slope, inputs, FIRST, preferred_element_type=F32)
        sums += jnp.sum(slope.astype(F32), axis=0, keepdims=True)
    chips, rows = sent_ref.shape[0], sent_ref.shape[1]
    part = half // chips
    feats = total.shape[1] // 2
    total = total.astype(BF16)
    tail = jnp.concatenate(
        [sums[:, k * LANES : (k + 1) * LANES] for k in range(half // LANES)]
        + [jnp.zeros((SUBLANES - half // LANES, LANES), F32)],
        axis=0,
    ).astype(BF16)
    for k in range(chips):
        here = slice(k * part, (k + 1) * part)
        sent_ref[k, :part, :] = total[here, :feats]
        sent_ref[k, part : 2 * part, :] = total[here, feats:]
        sent_ref[k, 2 * part : rows, :] = tail


def spread_kernel(got_ref, out_ref):
    total = jnp.sum(got_ref[...].astype(F32), axis=0).astype(BF16)
    for b in range(out_ref.shape[0]):
        out_ref[b] = total


def final_kernel(chip_ref, got_ref, self_ref, neigh_ref, bias_ref, sums_ref):
    part = self_ref.shape[0]
    total = jnp.sum(got_ref[...].astype(F32), axis=0)
    self_ref[...] = total[:part]
    neigh_ref[...] = total[part : 2 * part]
    sums_ref[...] = total[2 * part :]
    per_row = LANES // part
    row = sums_ref[pl.ds(chip_ref[0] // per_row, 1), :]
    lane = lax.broadcasted_iota(jnp.int32, (LANES, LANES), 0)
    to = lax.broadcasted_iota(jnp.int32, (LANES, LANES), 1)
    shift = chip_ref[0] % per_row * part
    moved = jnp.where(lane == to + shift, jnp.broadcast_to(row, (LANES, LANES)).T, 0.0)
    bias_ref[...] = jnp.sum(moved, axis=0, keepdims=True)[:, :part]


def local(
    features,
    tile_weights,
    tile_rows,
    tile_owners,
    tile_blocks,
    tile_counts,
    cotangent,
    w_self,
    w_neigh,
    bias,
):
    own = features[0].T
    width, node_count = own.shape
    slots, side = tile_weights.shape[1], tile_weights.shape[2]
    batches = lax.axis_size("dp")
    peers = lax.axis_size("x") * CORES
    chips = lax.axis_size("x") * DEPTH
    feats, hidden = w_self.shape
    nodes_here = cotangent.shape[1]
    row_blocks = nodes_here // side
    core = lax.axis_index("core")
    chip = lax.axis_index("x") * DEPTH + lax.axis_index("z")
    core_at, chip_at = core[None], chip[None]
    swap = [(i, CORES - 1 - i) for i in range(CORES)]

    whole = lax.all_to_all(
        jnp.broadcast_to(own[None], (DEPTH, width, node_count)),
        "z",
        split_axis=0,
        concat_axis=0,
        tiled=True,
    )
    half = hidden // CORES
    part = half // chips
    live = jnp.arange(slots, dtype=jnp.int32) < tile_counts[0, 0]
    rows_live = jnp.where(live, tile_rows[0], -1)
    cot, away, weights, half_bias, masked = call(
        functools.partial(split_kernel, part),
        (
            jax.ShapeDtypeStruct((nodes_here, half), BF16),
            jax.ShapeDtypeStruct((nodes_here, half), BF16),
            jax.ShapeDtypeStruct((2 * feats, half), BF16),
            jax.ShapeDtypeStruct((1, half), F32),
            jax.ShapeDtypeStruct((row_blocks * side, slots * side), BF16),
        ),
        [SMEM] + [VMEM] * 4 + [SMEM, VMEM],
        12,
    )(core_at, cotangent[0], w_self, w_neigh, bias[None], rows_live, tile_weights[0])
    their_cot = lax.ppermute(away, "core", swap)
    named = tile_owners[0, :, 0] * row_blocks + tile_blocks[0]
    held = (chip * CORES + core) * row_blocks + jnp.arange(row_blocks, dtype=jnp.int32)
    names = jnp.pad(jnp.concatenate([named, held]), (0, LANES - slots - row_blocks))
    names = names[None]
    pair = jnp.concatenate([names, lax.ppermute(names, "core", swap)], axis=0)
    reach = lax.axis_size("x")
    lists = [pair] + [
        lax.ppermute(pair, "x", [(i, (i + step) % reach) for i in range(reach)])
        for step in range(1, reach)
    ]
    sent = call(
        pack_kernel,
        jax.ShapeDtypeStruct((peers, DEPTH * width, (slots + row_blocks) * side), BF16),
        [SMEM] * (1 + reach) + [VMEM],
        8,
    )(jnp.stack([lax.axis_index("x"), core]), *lists, whole)
    got = lax.all_to_all(
        sent, ("x", "core"), split_axis=0, concat_axis=0, tiled=True
    ).reshape(feats, (slots + row_blocks) * side)
    mine = call(
        functools.partial(gather_kernel, width),
        jax.ShapeDtypeStruct((nodes_here, 2 * feats), BF16),
        [VMEM, VMEM],
        12,
    )(got, masked)
    theirs = lax.ppermute(mine, "core", swap)
    rows = 2 * part + SUBLANES
    sums = call(
        layer_kernel,
        jax.ShapeDtypeStruct((chips, rows, feats), BF16),
        [VMEM] * 6,
        16,
    )(mine, theirs, cot, their_cot, weights, half_bias)
    parts = lax.all_to_all(sums, ("x", "z"), split_axis=0, concat_axis=0, tiled=True)
    spread = call(
        spread_kernel,
        jax.ShapeDtypeStruct((batches, rows, feats), BF16),
        [VMEM],
        4,
    )(parts)
    totals = lax.all_to_all(spread, "dp", split_axis=0, concat_axis=0, tiled=True)
    out_s, out_n, out_b = call(
        final_kernel,
        (
            jax.ShapeDtypeStruct((part, feats), F32),
            jax.ShapeDtypeStruct((part, feats), F32),
            jax.ShapeDtypeStruct((1, part), F32),
        ),
        [SMEM, VMEM],
        4,
        [pltpu.VMEM((SUBLANES, LANES), F32)],
    )(chip_at, totals)
    return (out_s.T, out_n.T, out_b[0])


def solution(mesh):
    batches, owners = mesh.devices.shape
    split = Mesh(
        mesh.devices.reshape(batches, owners // (DEPTH * CORES), DEPTH, CORES),
        ("dp", "x", "z", "core"),
    )
    feat = ("x", "z", "core")
    return jax.shard_map(
        local,
        mesh=split,
        in_specs=(
            P("dp", None, feat),
            P("dp", feat, None, None),
            P("dp", feat),
            P("dp", feat, None),
            P("dp", feat),
            P("dp", feat),
            P("dp", feat, None),
            P(),
            P(),
            P(),
        ),
        out_specs=(P(None, feat), P(None, feat), P(feat)),
        check_vma=False,
    )
```

```python
import functools

import jax
import jax.numpy as jnp
from jax import lax
from jax.experimental import pallas as pl
from jax.experimental.pallas import tpu as pltpu
from jax.sharding import Mesh, PartitionSpec as P

CORES, DEPTH = 2, 8
LANES, SUBLANES = 128, 8
BF16, F32 = jnp.bfloat16, jnp.float32
VMEM = pl.BlockSpec(memory_space=pltpu.VMEM)
SMEM = pl.BlockSpec(memory_space=pltpu.SMEM)
MIB = 1024 * 1024
FIRST = (((0,), (0,)), ((), ()))
LAST = (((1,), (1,)), ((), ()))


def call(kernel, outs, specs, mib, scratch=()):
    return pl.pallas_call(
        kernel,
        out_shape=outs,
        in_specs=specs,
        out_specs=jax.tree.map(lambda _: VMEM, outs),
        scratch_shapes=list(scratch),
        compiler_params=pltpu.CompilerParams(vmem_limit_bytes=mib * MIB),
    )


def copies_kernel(own_ref, out_ref):
    own = own_ref[...]
    for z in range(out_ref.shape[0]):
        out_ref[z] = own


def pack_kernel(at_ref, near_ref, far_ref, whole_ref, sent_ref, table_ref):
    depth, width = whole_ref.shape[0], whole_ref.shape[1]
    for z in range(depth):
        table_ref[z * width : (z + 1) * width, :] = whole_ref[z]
    half = near_ref.shape[0]
    for row in range(2 * half):
        lists_ref = near_ref if row < half else far_ref
        p = jnp.bitwise_xor(at_ref[0], row)
        for s in range(sent_ref.shape[2] // LANES):
            at = pl.ds(pl.multiple_of(lists_ref[row % half, s] * LANES, LANES), LANES)
            sent_ref[p, :, s * LANES : (s + 1) * LANES] = table_ref[:, at]


def gather_kernel(width, got_ref, masked_ref, inputs_ref):
    feats = got_ref.shape[0]
    named = masked_ref.shape[1]
    agg = lax.dot_general(
        got_ref[:, :named],
        masked_ref[...],
        LAST,
        preferred_element_type=F32,
    ).astype(BF16)
    row = lax.broadcasted_iota(jnp.int32, (feats, feats), 0)
    feature = lax.broadcasted_iota(jnp.int32, (feats, feats), 1)
    column = row % width
    z = row // width % DEPTH
    core = row // (width * DEPTH) % CORES
    x = row // (width * DEPTH * CORES)
    place = ((x * DEPTH + z) * CORES + core) * width + column
    order = jnp.where(place == feature, 1.0, 0.0).astype(BF16)
    for k, value in enumerate((got_ref[:, named:], agg)):
        inputs_ref[:, k * feats : (k + 1) * feats] = lax.dot_general(
            value, order, FIRST, preferred_element_type=F32
        ).astype(BF16)


def split_kernel(
    part,
    core_ref,
    cot_ref,
    w_self_ref,
    w_neigh_ref,
    bias_ref,
    rows_ref,
    tiles_ref,
    mine_ref,
    theirs_ref,
    weights_ref,
    half_bias_ref,
    masked_ref,
):
    slots, side = tiles_ref.shape[0], tiles_ref.shape[1]
    for s in range(slots):
        tile = tiles_ref[s]
        for r in range(masked_ref.shape[0] // side):
            masked_ref[r * side : (r + 1) * side, s * side : (s + 1) * side] = jnp.where(
                rows_ref[s] == r, tile, jnp.zeros_like(tile)
            )
    pair = CORES * LANES
    lane = lax.broadcasted_iota(jnp.int32, (pair, LANES), 0)
    to = lax.broadcasted_iota(jnp.int32, (pair, LANES), 1)
    group = to // part * (CORES * part) + to % part
    here = jnp.where(lane == group + core_ref[0] * part, 1.0, 0.0)
    there = jnp.where(lane == group + (1 - core_ref[0]) * part, 1.0, 0.0)
    here16, there16 = here.astype(BF16), there.astype(BF16)
    feats = w_self_ref.shape[0]

    def pick(value, chosen):
        return jnp.dot(value, chosen, preferred_element_type=F32).astype(BF16)

    for m in range(mine_ref.shape[1] // LANES):
        out = slice(m * LANES, (m + 1) * LANES)
        wide = slice(m * pair, (m + 1) * pair)
        mine_ref[:, out] = pick(cot_ref[:, wide], here16)
        theirs_ref[:, out] = pick(cot_ref[:, wide], there16)
        weights_ref[:feats, out] = pick(w_self_ref[:, wide], here16)
        weights_ref[feats:, out] = pick(w_neigh_ref[:, wide], here16)
        half_bias_ref[:, out] = jnp.dot(
            jnp.broadcast_to(bias_ref[:, wide], (SUBLANES, pair)),
            here,
            precision=lax.Precision.HIGHEST,
            preferred_element_type=F32,
        )[:1]


def layer_kernel(
    mine_ref, theirs_ref, cot_ref, their_cot_ref, weights_ref, bias_ref, sent_ref
):
    half = cot_ref.shape[1]
    weights, bias = weights_ref[...], bias_ref[...]
    total, sums = 0.0, 0.0
    for inputs, cot in (
        (mine_ref[...], cot_ref[...]),
        (theirs_ref[...], their_cot_ref[...]),
    ):
        pre = jnp.dot(inputs, weights, preferred_element_type=F32) + bias
        s = jax.nn.sigmoid(pre)
        slope = (cot.astype(F32) * (s * (1.0 + pre * (1.0 - s)))).astype(BF16)
        total += lax.dot_general(slope, inputs, FIRST, preferred_element_type=F32)
        sums += jnp.sum(slope.astype(F32), axis=0, keepdims=True)
    chips, rows = sent_ref.shape[0], sent_ref.shape[1]
    part = half // chips
    feats = total.shape[1] // 2
    total = total.astype(BF16)
    tail = jnp.concatenate(
        [sums[:, k * LANES : (k + 1) * LANES] for k in range(half // LANES)]
        + [jnp.zeros((SUBLANES - half // LANES, LANES), F32)],
        axis=0,
    ).astype(BF16)
    for k in range(chips):
        here = slice(k * part, (k + 1) * part)
        sent_ref[k, :part, :] = total[here, :feats]
        sent_ref[k, part : 2 * part, :] = total[here, feats:]
        sent_ref[k, 2 * part : rows, :] = tail


def spread_kernel(got_ref, out_ref):
    total = jnp.sum(got_ref[...].astype(F32), axis=0).astype(BF16)
    for b in range(out_ref.shape[0]):
        out_ref[b] = total


def final_kernel(chip_ref, got_ref, self_ref, neigh_ref, bias_ref, sums_ref):
    part = self_ref.shape[0]
    total = jnp.sum(got_ref[...].astype(F32), axis=0)
    self_ref[...] = total[:part]
    neigh_ref[...] = total[part : 2 * part]
    sums_ref[...] = total[2 * part :]
    per_row = LANES // part
    row = sums_ref[pl.ds(chip_ref[0] // per_row, 1), :]
    lane = lax.broadcasted_iota(jnp.int32, (LANES, LANES), 0)
    to = lax.broadcasted_iota(jnp.int32, (LANES, LANES), 1)
    shift = chip_ref[0] % per_row * part
    moved = jnp.where(lane == to + shift, jnp.broadcast_to(row, (LANES, LANES)).T, 0.0)
    bias_ref[...] = jnp.sum(moved, axis=0, keepdims=True)[:, :part]


def local(
    features,
    tile_weights,
    tile_rows,
    tile_owners,
    tile_blocks,
    tile_counts,
    cotangent,
    w_self,
    w_neigh,
    bias,
):
    own = features[0].T
    width, node_count = own.shape
    slots, side = tile_weights.shape[1], tile_weights.shape[2]
    batches = lax.axis_size("dp")
    peers = lax.axis_size("x") * CORES
    chips = lax.axis_size("x") * DEPTH
    feats, hidden = w_self.shape
    nodes_here = cotangent.shape[1]
    row_blocks = nodes_here // side
    core = lax.axis_index("core")
    chip = lax.axis_index("x") * DEPTH + lax.axis_index("z")
    core_at, chip_at = core[None], chip[None]
    swap = [(i, CORES - 1 - i) for i in range(CORES)]

    copies = call(
        copies_kernel,
        jax.ShapeDtypeStruct((DEPTH, width, node_count), BF16),
        [VMEM],
        2,
    )(own)
    whole = lax.all_to_all(copies, "z", split_axis=0, concat_axis=0, tiled=True)
    half = hidden // CORES
    part = half // chips
    live = jnp.arange(slots, dtype=jnp.int32) < tile_counts[0, 0]
    rows_live = jnp.where(live, tile_rows[0], -1)
    cot, away, weights, half_bias, masked = call(
        functools.partial(split_kernel, part),
        (
            jax.ShapeDtypeStruct((nodes_here, half), BF16),
            jax.ShapeDtypeStruct((nodes_here, half), BF16),
            jax.ShapeDtypeStruct((2 * feats, half), BF16),
            jax.ShapeDtypeStruct((1, half), F32),
            jax.ShapeDtypeStruct((row_blocks * side, slots * side), BF16),
        ),
        [SMEM] + [VMEM] * 4 + [SMEM, VMEM],
        12,
    )(core_at, cotangent[0], w_self, w_neigh, bias[None], rows_live, tile_weights[0])
    their_cot = lax.ppermute(away, "core", swap)
    named = tile_owners[0, :, 0] * row_blocks + tile_blocks[0]
    held = (chip * CORES + core) * row_blocks + jnp.arange(row_blocks, dtype=jnp.int32)
    names = jnp.pad(jnp.concatenate([named, held]), (0, LANES - slots - row_blocks))
    near = names[None]
    far = lax.ppermute(near, "core", swap)
    reach = lax.axis_size("x")
    step = 1
    while step < reach:
        near = jnp.concatenate([near, far], axis=0)
        far = lax.ppermute(near, "x", [(i, i ^ step) for i in range(reach)])
        step *= 2
    columns = DEPTH * width
    sent = call(
        pack_kernel,
        jax.ShapeDtypeStruct((peers, columns, (slots + row_blocks) * side), BF16),
        [SMEM, SMEM, SMEM, VMEM],
        8,
        [pltpu.VMEM((columns, node_count), BF16)],
    )((lax.axis_index("x") * CORES + core)[None], near, far, whole)
    got = lax.all_to_all(
        sent, ("x", "core"), split_axis=0, concat_axis=0, tiled=True
    ).reshape(feats, (slots + row_blocks) * side)
    mine = call(
        functools.partial(gather_kernel, width),
        jax.ShapeDtypeStruct((nodes_here, 2 * feats), BF16),
        [VMEM, VMEM],
        12,
    )(got, masked)
    theirs = lax.ppermute(mine, "core", swap)
    rows = 2 * part + SUBLANES
    sums = call(
        layer_kernel,
        jax.ShapeDtypeStruct((chips, rows, feats), BF16),
        [VMEM] * 6,
        16,
    )(mine, theirs, cot, their_cot, weights, half_bias)
    parts = lax.all_to_all(sums, ("x", "z"), split_axis=0, concat_axis=0, tiled=True)
    spread = call(
        spread_kernel,
        jax.ShapeDtypeStruct((batches, rows, feats), BF16),
        [VMEM],
        4,
    )(parts)
    totals = lax.all_to_all(spread, "dp", split_axis=0, concat_axis=0, tiled=True)
    out_s, out_n, out_b = call(
        final_kernel,
        (
            jax.ShapeDtypeStruct((part, feats), F32),
            jax.ShapeDtypeStruct((part, feats), F32),
            jax.ShapeDtypeStruct((1, part), F32),
        ),
        [SMEM, VMEM],
        4,
        [pltpu.VMEM((SUBLANES, LANES), F32)],
    )(chip_at, totals)
    return (out_s.T, out_n.T, out_b[0])


def solution(mesh):
    batches, owners = mesh.devices.shape
    split = Mesh(
        mesh.devices.reshape(batches, owners // (DEPTH * CORES), DEPTH, CORES),
        ("dp", "x", "z", "core"),
    )
    feat = ("x", "z", "core")
    return jax.shard_map(
        local,
        mesh=split,
        in_specs=(
            P("dp", None, feat),
            P("dp", feat, None, None),
            P("dp", feat),
            P("dp", feat, None),
            P("dp", feat),
            P("dp", feat),
            P("dp", feat, None),
            P(),
            P(),
            P(),
        ),
        out_specs=(P(None, feat), P(None, feat), P(feat)),
        check_vma=False,
    )
```

```python
import functools

import jax
import jax.numpy as jnp
from jax import lax
from jax.experimental import pallas as pl
from jax.experimental.pallas import tpu as pltpu
from jax.sharding import Mesh, PartitionSpec as P

CORES, DEPTH = 2, 8
LANES, SUBLANES = 128, 8
BF16, F32 = jnp.bfloat16, jnp.float32
VMEM = pl.BlockSpec(memory_space=pltpu.VMEM)
SMEM = pl.BlockSpec(memory_space=pltpu.SMEM)
HBM = pl.BlockSpec(memory_space=pltpu.HBM)
MIB = 1024 * 1024
FIRST = (((0,), (0,)), ((), ()))
LAST = (((1,), (1,)), ((), ()))


def call(kernel, outs, specs, mib, scratch=(), out_spec=VMEM):
    return pl.pallas_call(
        kernel,
        out_shape=outs,
        in_specs=specs,
        out_specs=jax.tree.map(lambda _: out_spec, outs),
        scratch_shapes=list(scratch),
        compiler_params=pltpu.CompilerParams(vmem_limit_bytes=mib * MIB),
    )


def copies_kernel(own_ref, out_ref, sems):
    copies = [
        pltpu.make_async_copy(own_ref, out_ref.at[z], sems.at[z])
        for z in range(out_ref.shape[0])
    ]
    for copy in copies:
        copy.start()
    for copy in copies:
        copy.wait()


def pack_kernel(at_ref, near_ref, far_ref, whole_ref, sent_ref, table_ref):
    depth, width = whole_ref.shape[0], whole_ref.shape[1]
    for z in range(depth):
        table_ref[z * width : (z + 1) * width, :] = whole_ref[z]
    half = near_ref.shape[0]
    for row in range(2 * half):
        lists_ref = near_ref if row < half else far_ref
        differs, k = row % CORES, 1
        while row >> k:
            differs ^= (row >> k) % 2 * ((1 << k) - 1) * CORES
            k += 1
        p = jnp.bitwise_xor(at_ref[0], differs)
        for s in range(sent_ref.shape[2] // LANES):
            at = pl.ds(pl.multiple_of(lists_ref[row % half, s] * LANES, LANES), LANES)
            sent_ref[p, :, s * LANES : (s + 1) * LANES] = table_ref[:, at]


def gather_kernel(width, got_ref, masked_ref, inputs_ref):
    feats = got_ref.shape[0]
    named = masked_ref.shape[1]
    agg = lax.dot_general(
        got_ref[:, :named],
        masked_ref[...],
        LAST,
        preferred_element_type=F32,
    ).astype(BF16)
    row = lax.broadcasted_iota(jnp.int32, (feats, feats), 0)
    feature = lax.broadcasted_iota(jnp.int32, (feats, feats), 1)
    column = row % width
    z = row // width % DEPTH
    core = row // (width * DEPTH) % CORES
    x = row // (width * DEPTH * CORES)
    place = ((x * DEPTH + z) * CORES + core) * width + column
    order = jnp.where(place == feature, 1.0, 0.0).astype(BF16)
    for k, value in enumerate((got_ref[:, named:], agg)):
        inputs_ref[:, k * feats : (k + 1) * feats] = lax.dot_general(
            value, order, FIRST, preferred_element_type=F32
        ).astype(BF16)


def split_kernel(
    part,
    core_ref,
    cot_ref,
    w_self_ref,
    w_neigh_ref,
    bias_ref,
    rows_ref,
    tiles_ref,
    mine_ref,
    theirs_ref,
    weights_ref,
    half_bias_ref,
    masked_ref,
):
    slots, side = tiles_ref.shape[0], tiles_ref.shape[1]
    for s in range(slots):
        tile = tiles_ref[s]
        for r in range(masked_ref.shape[0] // side):
            masked_ref[r * side : (r + 1) * side, s * side : (s + 1) * side] = jnp.where(
                rows_ref[s] == r, tile, jnp.zeros_like(tile)
            )
    pair = CORES * LANES
    lane = lax.broadcasted_iota(jnp.int32, (pair, LANES), 0)
    to = lax.broadcasted_iota(jnp.int32, (pair, LANES), 1)
    group = to // part * (CORES * part) + to % part
    here = jnp.where(lane == group + core_ref[0] * part, 1.0, 0.0)
    there = jnp.where(lane == group + (1 - core_ref[0]) * part, 1.0, 0.0)
    here16, there16 = here.astype(BF16), there.astype(BF16)
    feats = w_self_ref.shape[0]

    def pick(value, chosen):
        return jnp.dot(value, chosen, preferred_element_type=F32).astype(BF16)

    for m in range(mine_ref.shape[1] // LANES):
        out = slice(m * LANES, (m + 1) * LANES)
        wide = slice(m * pair, (m + 1) * pair)
        mine_ref[:, out] = pick(cot_ref[:, wide], here16)
        theirs_ref[:, out] = pick(cot_ref[:, wide], there16)
        weights_ref[:feats, out] = pick(w_self_ref[:, wide], here16)
        weights_ref[feats:, out] = pick(w_neigh_ref[:, wide], here16)
        half_bias_ref[:, out] = jnp.dot(
            jnp.broadcast_to(bias_ref[:, wide], (SUBLANES, pair)),
            here,
            precision=lax.Precision.HIGHEST,
            preferred_element_type=F32,
        )[:1]


def layer_kernel(
    mine_ref, theirs_ref, cot_ref, their_cot_ref, weights_ref, bias_ref, sent_ref
):
    half = cot_ref.shape[1]
    weights, bias = weights_ref[...], bias_ref[...]
    total, sums = 0.0, 0.0
    for inputs, cot in (
        (mine_ref[...], cot_ref[...]),
        (theirs_ref[...], their_cot_ref[...]),
    ):
        pre = jnp.dot(inputs, weights, preferred_element_type=F32) + bias
        s = jax.nn.sigmoid(pre)
        slope = (cot.astype(F32) * (s * (1.0 + pre * (1.0 - s)))).astype(BF16)
        total += lax.dot_general(slope, inputs, FIRST, preferred_element_type=F32)
        sums += jnp.sum(slope.astype(F32), axis=0, keepdims=True)
    chips, rows = sent_ref.shape[0], sent_ref.shape[1]
    part = half // chips
    feats = total.shape[1] // 2
    total = total.astype(BF16)
    tail = jnp.concatenate(
        [sums[:, k * LANES : (k + 1) * LANES] for k in range(half // LANES)]
        + [jnp.zeros((SUBLANES - half // LANES, LANES), F32)],
        axis=0,
    ).astype(BF16)
    for k in range(chips):
        here = slice(k * part, (k + 1) * part)
        sent_ref[k, :part, :] = total[here, :feats]
        sent_ref[k, part : 2 * part, :] = total[here, feats:]
        sent_ref[k, 2 * part : rows, :] = tail


def spread_kernel(got_ref, out_ref):
    total = jnp.sum(got_ref[...].astype(F32), axis=0).astype(BF16)
    for b in range(out_ref.shape[0]):
        out_ref[b] = total


def final_kernel(chip_ref, got_ref, self_ref, neigh_ref, bias_ref, sums_ref):
    part = self_ref.shape[0]
    total = jnp.sum(got_ref[...].astype(F32), axis=0)
    self_ref[...] = total[:part]
    neigh_ref[...] = total[part : 2 * part]
    sums_ref[...] = total[2 * part :]
    per_row = LANES // part
    row = sums_ref[pl.ds(chip_ref[0] // per_row, 1), :]
    lane = lax.broadcasted_iota(jnp.int32, (LANES, LANES), 0)
    to = lax.broadcasted_iota(jnp.int32, (LANES, LANES), 1)
    shift = chip_ref[0] % per_row * part
    moved = jnp.where(lane == to + shift, jnp.broadcast_to(row, (LANES, LANES)).T, 0.0)
    bias_ref[...] = jnp.sum(moved, axis=0, keepdims=True)[:, :part]


def local(
    features,
    tile_weights,
    tile_rows,
    tile_owners,
    tile_blocks,
    tile_counts,
    cotangent,
    w_self,
    w_neigh,
    bias,
):
    own = features[0].T
    width, node_count = own.shape
    slots, side = tile_weights.shape[1], tile_weights.shape[2]
    batches = lax.axis_size("dp")
    peers = lax.axis_size("x") * CORES
    chips = lax.axis_size("x") * DEPTH
    feats, hidden = w_self.shape
    nodes_here = cotangent.shape[1]
    row_blocks = nodes_here // side
    core = lax.axis_index("core")
    chip = lax.axis_index("x") * DEPTH + lax.axis_index("z")
    core_at, chip_at = core[None], chip[None]
    swap = [(i, CORES - 1 - i) for i in range(CORES)]

    copies = call(
        copies_kernel,
        jax.ShapeDtypeStruct((DEPTH, width, node_count), BF16),
        [HBM],
        60,
        [pltpu.SemaphoreType.DMA((DEPTH,))],
        HBM,
    )(own)
    whole = lax.all_to_all(copies, "z", split_axis=0, concat_axis=0, tiled=True)
    half = hidden // CORES
    part = half // chips
    live = jnp.arange(slots, dtype=jnp.int32) < tile_counts[0, 0]
    rows_live = jnp.where(live, tile_rows[0], -1)
    cot, away, weights, half_bias, masked = call(
        functools.partial(split_kernel, part),
        (
            jax.ShapeDtypeStruct((nodes_here, half), BF16),
            jax.ShapeDtypeStruct((nodes_here, half), BF16),
            jax.ShapeDtypeStruct((2 * feats, half), BF16),
            jax.ShapeDtypeStruct((1, half), F32),
            jax.ShapeDtypeStruct((row_blocks * side, slots * side), BF16),
        ),
        [SMEM] + [VMEM] * 4 + [SMEM, VMEM],
        12,
    )(core_at, cotangent[0], w_self, w_neigh, bias[None], rows_live, tile_weights[0])
    their_cot = lax.ppermute(away, "core", swap)
    named = tile_owners[0, :, 0] * row_blocks + tile_blocks[0]
    held = (chip * CORES + core) * row_blocks + jnp.arange(row_blocks, dtype=jnp.int32)
    names = jnp.pad(jnp.concatenate([named, held]), (0, LANES - slots - row_blocks))
    near = names[None]
    far = lax.ppermute(near, "core", swap)
    reach = lax.axis_size("x")
    step = 1
    while step < reach:
        near = jnp.concatenate([near, far], axis=0)
        far = lax.ppermute(near, "x", [(i, i ^ (2 * step - 1)) for i in range(reach)])
        step *= 2
    columns = DEPTH * width
    sent = call(
        pack_kernel,
        jax.ShapeDtypeStruct((peers, columns, (slots + row_blocks) * side), BF16),
        [SMEM, SMEM, SMEM, VMEM],
        8,
        [pltpu.VMEM((columns, node_count), BF16)],
    )((lax.axis_index("x") * CORES + core)[None], near, far, whole)
    got = lax.all_to_all(
        sent, ("x", "core"), split_axis=0, concat_axis=0, tiled=True
    ).reshape(feats, (slots + row_blocks) * side)
    mine = call(
        functools.partial(gather_kernel, width),
        jax.ShapeDtypeStruct((nodes_here, 2 * feats), BF16),
        [VMEM, VMEM],
        12,
    )(got, masked)
    theirs = lax.ppermute(mine, "core", swap)
    rows = 2 * part + SUBLANES
    sums = call(
        layer_kernel,
        jax.ShapeDtypeStruct((chips, rows, feats), BF16),
        [VMEM] * 6,
        16,
    )(mine, theirs, cot, their_cot, weights, half_bias)
    parts = lax.all_to_all(sums, ("x", "z"), split_axis=0, concat_axis=0, tiled=True)
    spread = call(
        spread_kernel,
        jax.ShapeDtypeStruct((batches, rows, feats), BF16),
        [VMEM],
        4,
    )(parts)
    totals = lax.all_to_all(spread, "dp", split_axis=0, concat_axis=0, tiled=True)
    out_s, out_n, out_b = call(
        final_kernel,
        (
            jax.ShapeDtypeStruct((part, feats), F32),
            jax.ShapeDtypeStruct((part, feats), F32),
            jax.ShapeDtypeStruct((1, part), F32),
        ),
        [SMEM, VMEM],
        4,
        [pltpu.VMEM((SUBLANES, LANES), F32)],
    )(chip_at, totals)
    return (out_s.T, out_n.T, out_b[0])


def solution(mesh):
    batches, owners = mesh.devices.shape
    split = Mesh(
        mesh.devices.reshape(batches, owners // (DEPTH * CORES), DEPTH, CORES),
        ("dp", "x", "z", "core"),
    )
    feat = ("x", "z", "core")
    return jax.shard_map(
        local,
        mesh=split,
        in_specs=(
            P("dp", None, feat),
            P("dp", feat, None, None),
            P("dp", feat),
            P("dp", feat, None),
            P("dp", feat),
            P("dp", feat),
            P("dp", feat, None),
            P(),
            P(),
            P(),
        ),
        out_specs=(P(None, feat), P(None, feat), P(feat)),
        check_vma=False,
    )
```

```python
import functools

import jax
import jax.numpy as jnp
from jax import lax
from jax.experimental import pallas as pl
from jax.experimental.pallas import tpu as pltpu
from jax.sharding import Mesh, PartitionSpec as P

CORES, DEPTH = 2, 8
LANES, SUBLANES = 128, 8
BF16, F32 = jnp.bfloat16, jnp.float32
VMEM = pl.BlockSpec(memory_space=pltpu.VMEM)
SMEM = pl.BlockSpec(memory_space=pltpu.SMEM)
MIB = 1024 * 1024
FIRST = (((0,), (0,)), ((), ()))
LAST = (((1,), (1,)), ((), ()))


def call(kernel, outs, specs, mib, scratch=()):
    return pl.pallas_call(
        kernel,
        out_shape=outs,
        in_specs=specs,
        out_specs=jax.tree.map(lambda _: VMEM, outs),
        scratch_shapes=list(scratch),
        compiler_params=pltpu.CompilerParams(vmem_limit_bytes=mib * MIB),
    )


def copies_kernel(own_ref, out_ref):
    own = own_ref[...]
    for z in range(out_ref.shape[0]):
        out_ref[z] = own


def pack_kernel(lists_ref, whole_ref, sent_ref, table_ref):
    depth, width = whole_ref.shape[0], whole_ref.shape[1]
    for z in range(depth):
        table_ref[z * width : (z + 1) * width, :] = whole_ref[z]
    for p in range(sent_ref.shape[0]):
        for s in range(sent_ref.shape[2] // LANES):
            at = pl.ds(pl.multiple_of(lists_ref[p, s] * LANES, LANES), LANES)
            sent_ref[p, :, s * LANES : (s + 1) * LANES] = table_ref[:, at]


def gather_kernel(width, got_ref, masked_ref, inputs_ref):
    feats = got_ref.shape[0]
    named = masked_ref.shape[1]
    agg = lax.dot_general(
        got_ref[:, :named],
        masked_ref[...],
        LAST,
        preferred_element_type=F32,
    ).astype(BF16)
    row = lax.broadcasted_iota(jnp.int32, (feats, feats), 0)
    feature = lax.broadcasted_iota(jnp.int32, (feats, feats), 1)
    column = row % width
    z = row // width % DEPTH
    core = row // (width * DEPTH) % CORES
    x = row // (width * DEPTH * CORES)
    place = ((x * DEPTH + z) * CORES + core) * width + column
    order = jnp.where(place == feature, 1.0, 0.0).astype(BF16)
    for k, value in enumerate((got_ref[:, named:], agg)):
        inputs_ref[:, k * feats : (k + 1) * feats] = lax.dot_general(
            value, order, FIRST, preferred_element_type=F32
        ).astype(BF16)


def split_kernel(
    part,
    core_ref,
    cot_ref,
    w_self_ref,
    w_neigh_ref,
    bias_ref,
    rows_ref,
    tiles_ref,
    mine_ref,
    theirs_ref,
    weights_ref,
    half_bias_ref,
    masked_ref,
):
    slots, side = tiles_ref.shape[0], tiles_ref.shape[1]
    for s in range(slots):
        tile = tiles_ref[s]
        for r in range(masked_ref.shape[0] // side):
            masked_ref[r * side : (r + 1) * side, s * side : (s + 1) * side] = jnp.where(
                rows_ref[s] == r, tile, jnp.zeros_like(tile)
            )
    pair = CORES * LANES
    lane = lax.broadcasted_iota(jnp.int32, (pair, LANES), 0)
    to = lax.broadcasted_iota(jnp.int32, (pair, LANES), 1)
    group = to // part * (CORES * part) + to % part
    here = jnp.where(lane == group + core_ref[0] * part, 1.0, 0.0)
    there = jnp.where(lane == group + (1 - core_ref[0]) * part, 1.0, 0.0)
    here16, there16 = here.astype(BF16), there.astype(BF16)
    feats = w_self_ref.shape[0]

    def pick(value, chosen):
        return jnp.dot(value, chosen, preferred_element_type=F32).astype(BF16)

    for m in range(mine_ref.shape[1] // LANES):
        out = slice(m * LANES, (m + 1) * LANES)
        wide = slice(m * pair, (m + 1) * pair)
        mine_ref[:, out] = pick(cot_ref[:, wide], here16)
        theirs_ref[:, out] = pick(cot_ref[:, wide], there16)
        weights_ref[:feats, out] = pick(w_self_ref[:, wide], here16)
        weights_ref[feats:, out] = pick(w_neigh_ref[:, wide], here16)
        half_bias_ref[:, out] = jnp.dot(
            jnp.broadcast_to(bias_ref[:, wide], (SUBLANES, pair)),
            here,
            precision=lax.Precision.HIGHEST,
            preferred_element_type=F32,
        )[:1]


def layer_kernel(
    mine_ref, theirs_ref, cot_ref, their_cot_ref, weights_ref, bias_ref, sent_ref
):
    half = cot_ref.shape[1]
    weights, bias = weights_ref[...], bias_ref[...]
    total, sums = 0.0, 0.0
    for inputs, cot in (
        (mine_ref[...], cot_ref[...]),
        (theirs_ref[...], their_cot_ref[...]),
    ):
        pre = jnp.dot(inputs, weights, preferred_element_type=F32) + bias
        s = jax.nn.sigmoid(pre)
        slope = (cot.astype(F32) * (s * (1.0 + pre * (1.0 - s)))).astype(BF16)
        total += lax.dot_general(slope, inputs, FIRST, preferred_element_type=F32)
        sums += jnp.sum(slope.astype(F32), axis=0, keepdims=True)
    chips, rows = sent_ref.shape[0], sent_ref.shape[1]
    part = half // chips
    feats = total.shape[1] // 2
    total = total.astype(BF16)
    tail = jnp.concatenate(
        [sums[:, k * LANES : (k + 1) * LANES] for k in range(half // LANES)]
        + [jnp.zeros((SUBLANES - half // LANES, LANES), F32)],
        axis=0,
    ).astype(BF16)
    for k in range(chips):
        here = slice(k * part, (k + 1) * part)
        sent_ref[k, :part, :] = total[here, :feats]
        sent_ref[k, part : 2 * part, :] = total[here, feats:]
        sent_ref[k, 2 * part : rows, :] = tail


def spread_kernel(got_ref, out_ref):
    total = jnp.sum(got_ref[...].astype(F32), axis=0).astype(BF16)
    for b in range(out_ref.shape[0]):
        out_ref[b] = total


def final_kernel(chip_ref, got_ref, self_ref, neigh_ref, bias_ref, sums_ref):
    part = self_ref.shape[0]
    total = jnp.sum(got_ref[...].astype(F32), axis=0)
    self_ref[...] = total[:part]
    neigh_ref[...] = total[part : 2 * part]
    sums_ref[...] = total[2 * part :]
    per_row = LANES // part
    row = sums_ref[pl.ds(chip_ref[0] // per_row, 1), :]
    lane = lax.broadcasted_iota(jnp.int32, (LANES, LANES), 0)
    to = lax.broadcasted_iota(jnp.int32, (LANES, LANES), 1)
    shift = chip_ref[0] % per_row * part
    moved = jnp.where(lane == to + shift, jnp.broadcast_to(row, (LANES, LANES)).T, 0.0)
    bias_ref[...] = jnp.sum(moved, axis=0, keepdims=True)[:, :part]


def local(
    features,
    tile_weights,
    tile_rows,
    tile_owners,
    tile_blocks,
    tile_counts,
    cotangent,
    w_self,
    w_neigh,
    bias,
):
    own = features[0].T
    width, node_count = own.shape
    slots, side = tile_weights.shape[1], tile_weights.shape[2]
    batches = lax.axis_size("dp")
    peers = lax.axis_size("x") * CORES
    chips = lax.axis_size("x") * DEPTH
    feats, hidden = w_self.shape
    nodes_here = cotangent.shape[1]
    row_blocks = nodes_here // side
    core = lax.axis_index("core")
    chip = lax.axis_index("x") * DEPTH + lax.axis_index("z")
    core_at, chip_at = core[None], chip[None]
    swap = [(i, CORES - 1 - i) for i in range(CORES)]

    copies = call(
        copies_kernel,
        jax.ShapeDtypeStruct((DEPTH, width, node_count), BF16),
        [VMEM],
        60,
    )(own)
    whole = lax.all_to_all(copies, "z", split_axis=0, concat_axis=0, tiled=True)
    half = hidden // CORES
    part = half // chips
    live = jnp.arange(slots, dtype=jnp.int32) < tile_counts[0, 0]
    rows_live = jnp.where(live, tile_rows[0], -1)
    cot, away, weights, half_bias, masked = call(
        functools.partial(split_kernel, part),
        (
            jax.ShapeDtypeStruct((nodes_here, half), BF16),
            jax.ShapeDtypeStruct((nodes_here, half), BF16),
            jax.ShapeDtypeStruct((2 * feats, half), BF16),
            jax.ShapeDtypeStruct((1, half), F32),
            jax.ShapeDtypeStruct((row_blocks * side, slots * side), BF16),
        ),
        [SMEM] + [VMEM] * 4 + [SMEM, VMEM],
        12,
    )(core_at, cotangent[0], w_self, w_neigh, bias[None], rows_live, tile_weights[0])
    their_cot = lax.ppermute(away, "core", swap)
    named = tile_owners[0, :, 0] * row_blocks + tile_blocks[0]
    held = (chip * CORES + core) * row_blocks + jnp.arange(row_blocks, dtype=jnp.int32)
    names = jnp.pad(jnp.concatenate([named, held]), (0, LANES - slots - row_blocks))
    lists = lax.all_gather(names[None], ("x", "core"), axis=0, tiled=True)
    columns = DEPTH * width
    sent = call(
        pack_kernel,
        jax.ShapeDtypeStruct((peers, columns, (slots + row_blocks) * side), BF16),
        [SMEM, VMEM],
        8,
        [pltpu.VMEM((columns, node_count), BF16)],
    )(lists, whole)
    got = lax.all_to_all(
        sent, ("x", "core"), split_axis=0, concat_axis=0, tiled=True
    ).reshape(feats, (slots + row_blocks) * side)
    mine = call(
        functools.partial(gather_kernel, width),
        jax.ShapeDtypeStruct((nodes_here, 2 * feats), BF16),
        [VMEM, VMEM],
        12,
    )(got, masked)
    theirs = lax.ppermute(mine, "core", swap)
    rows = 2 * part + SUBLANES
    sums = call(
        layer_kernel,
        jax.ShapeDtypeStruct((chips, rows, feats), BF16),
        [VMEM] * 6,
        16,
    )(mine, theirs, cot, their_cot, weights, half_bias)
    parts = lax.all_to_all(sums, ("x", "z"), split_axis=0, concat_axis=0, tiled=True)
    spread = call(
        spread_kernel,
        jax.ShapeDtypeStruct((batches, rows, feats), BF16),
        [VMEM],
        4,
    )(parts)
    totals = lax.all_to_all(spread, "dp", split_axis=0, concat_axis=0, tiled=True)
    out_s, out_n, out_b = call(
        final_kernel,
        (
            jax.ShapeDtypeStruct((part, feats), F32),
            jax.ShapeDtypeStruct((part, feats), F32),
            jax.ShapeDtypeStruct((1, part), F32),
        ),
        [SMEM, VMEM],
        4,
        [pltpu.VMEM((SUBLANES, LANES), F32)],
    )(chip_at, totals)
    return (out_s.T, out_n.T, out_b[0])


def solution(mesh):
    batches, owners = mesh.devices.shape
    split = Mesh(
        mesh.devices.reshape(batches, owners // (DEPTH * CORES), DEPTH, CORES),
        ("dp", "x", "z", "core"),
    )
    feat = ("x", "z", "core")
    return jax.shard_map(
        local,
        mesh=split,
        in_specs=(
            P("dp", None, feat),
            P("dp", feat, None, None),
            P("dp", feat),
            P("dp", feat, None),
            P("dp", feat),
            P("dp", feat),
            P("dp", feat, None),
            P(),
            P(),
            P(),
        ),
        out_specs=(P(None, feat), P(None, feat), P(feat)),
        check_vma=False,
    )
```

```python
import functools

import jax
import jax.numpy as jnp
from jax import lax
from jax.experimental import pallas as pl
from jax.experimental.pallas import tpu as pltpu
from jax.sharding import Mesh, PartitionSpec as P

CORES, HIGH, LOW = 2, 4, 2
LANES, SUBLANES = 128, 8
BF16, F32 = jnp.bfloat16, jnp.float32
VMEM = pl.BlockSpec(memory_space=pltpu.VMEM)
SMEM = pl.BlockSpec(memory_space=pltpu.SMEM)
MIB = 1024 * 1024
FIRST = (((0,), (0,)), ((), ()))
LAST = (((1,), (1,)), ((), ()))


def call(kernel, outs, specs, mib, scratch=()):
    return pl.pallas_call(
        kernel,
        out_shape=outs,
        in_specs=specs,
        out_specs=jax.tree.map(lambda _: VMEM, outs),
        scratch_shapes=list(scratch),
        compiler_params=pltpu.CompilerParams(vmem_limit_bytes=mib * MIB),
    )


def copies_kernel(own_ref, out_ref):
    own = own_ref[...]
    for z in range(out_ref.shape[0]):
        out_ref[z] = own


def table_kernel(lists_ref, whole_ref, table_ref):
    del lists_ref
    high, width = whole_ref.shape[0], whole_ref.shape[1]
    for z in range(high):
        table_ref[z * width : (z + 1) * width, :] = whole_ref[z]


def pack_kernel(lists_ref, own_ref, other_ref, sent_ref):
    for p in range(sent_ref.shape[0]):
        for s in range(sent_ref.shape[2] // LANES):
            at = pl.ds(pl.multiple_of(lists_ref[p, s] * LANES, LANES), LANES)
            sent_ref[p, :, s * LANES : (s + 1) * LANES] = jnp.concatenate(
                [own_ref[:, at], other_ref[:, at]], axis=0
            )


def gather_kernel(width, core_ref, got_ref, masked_ref, inputs_ref):
    feats = got_ref.shape[0]
    named = masked_ref.shape[1]
    agg = lax.dot_general(
        got_ref[:, :named],
        masked_ref[...],
        LAST,
        preferred_element_type=F32,
    ).astype(BF16)
    row = lax.broadcasted_iota(jnp.int32, (feats, feats), 0)
    feature = lax.broadcasted_iota(jnp.int32, (feats, feats), 1)
    column, zh = row % width, row // width % HIGH
    rest = row // (width * HIGH)
    parity = jnp.bitwise_xor(rest % CORES, core_ref[0])
    reach = feats // (width * HIGH * CORES * LOW)
    x, zl = rest // CORES % reach, rest // (CORES * reach)
    place = (((x * HIGH + zh) * LOW + zl) * CORES + parity) * width + column
    order = jnp.where(place == feature, 1.0, 0.0).astype(BF16)
    for k, value in enumerate((got_ref[:, named:], agg)):
        inputs_ref[:, k * feats : (k + 1) * feats] = lax.dot_general(
            value, order, FIRST, preferred_element_type=F32
        ).astype(BF16)


def split_kernel(
    part,
    core_ref,
    cot_ref,
    w_self_ref,
    w_neigh_ref,
    bias_ref,
    rows_ref,
    tiles_ref,
    mine_ref,
    theirs_ref,
    weights_ref,
    half_bias_ref,
    masked_ref,
):
    slots, side = tiles_ref.shape[0], tiles_ref.shape[1]
    for s in range(slots):
        tile = tiles_ref[s]
        for r in range(masked_ref.shape[0] // side):
            masked_ref[r * side : (r + 1) * side, s * side : (s + 1) * side] = jnp.where(
                rows_ref[s] == r, tile, jnp.zeros_like(tile)
            )
    pair = CORES * LANES
    lane = lax.broadcasted_iota(jnp.int32, (pair, LANES), 0)
    to = lax.broadcasted_iota(jnp.int32, (pair, LANES), 1)
    group = to // part * (CORES * part) + to % part
    here = jnp.where(lane == group + core_ref[0] * part, 1.0, 0.0)
    there = jnp.where(lane == group + (1 - core_ref[0]) * part, 1.0, 0.0)
    here16, there16 = here.astype(BF16), there.astype(BF16)
    feats = w_self_ref.shape[0]

    def pick(value, chosen):
        return jnp.dot(value, chosen, preferred_element_type=F32).astype(BF16)

    for m in range(mine_ref.shape[1] // LANES):
        out = slice(m * LANES, (m + 1) * LANES)
        wide = slice(m * pair, (m + 1) * pair)
        mine_ref[:, out] = pick(cot_ref[:, wide], here16)
        theirs_ref[:, out] = pick(cot_ref[:, wide], there16)
        weights_ref[:feats, out] = pick(w_self_ref[:, wide], here16)
        weights_ref[feats:, out] = pick(w_neigh_ref[:, wide], here16)
        half_bias_ref[:, out] = jnp.dot(
            jnp.broadcast_to(bias_ref[:, wide], (SUBLANES, pair)),
            here,
            precision=lax.Precision.HIGHEST,
            preferred_element_type=F32,
        )[:1]


def layer_kernel(
    mine_ref, theirs_ref, cot_ref, their_cot_ref, weights_ref, bias_ref, sent_ref
):
    half = cot_ref.shape[1]
    weights, bias = weights_ref[...], bias_ref[...]
    total, sums = 0.0, 0.0
    for inputs, cot in (
        (mine_ref[...], cot_ref[...]),
        (theirs_ref[...], their_cot_ref[...]),
    ):
        pre = jnp.dot(inputs, weights, preferred_element_type=F32) + bias
        s = jax.nn.sigmoid(pre)
        slope = (cot.astype(F32) * (s * (1.0 + pre * (1.0 - s)))).astype(BF16)
        total += lax.dot_general(slope, inputs, FIRST, preferred_element_type=F32)
        sums += jnp.sum(slope.astype(F32), axis=0, keepdims=True)
    chips, rows = sent_ref.shape[0], sent_ref.shape[1]
    part = half // chips
    feats = total.shape[1] // 2
    total = total.astype(BF16)
    tail = jnp.concatenate(
        [sums[:, k * LANES : (k + 1) * LANES] for k in range(half // LANES)]
        + [jnp.zeros((SUBLANES - half // LANES, LANES), F32)],
        axis=0,
    ).astype(BF16)
    for k in range(chips):
        here = slice(k * part, (k + 1) * part)
        sent_ref[k, :part, :] = total[here, :feats]
        sent_ref[k, part : 2 * part, :] = total[here, feats:]
        sent_ref[k, 2 * part : rows, :] = tail


def spread_kernel(got_ref, out_ref):
    total = jnp.sum(got_ref[...].astype(F32), axis=0).astype(BF16)
    for b in range(out_ref.shape[0]):
        out_ref[b] = total


def final_kernel(chip_ref, got_ref, self_ref, neigh_ref, bias_ref, sums_ref):
    part = self_ref.shape[0]
    total = jnp.sum(got_ref[...].astype(F32), axis=0)
    self_ref[...] = total[:part]
    neigh_ref[...] = total[part : 2 * part]
    sums_ref[...] = total[2 * part :]
    per_row = LANES // part
    row = sums_ref[pl.ds(chip_ref[0] // per_row, 1), :]
    lane = lax.broadcasted_iota(jnp.int32, (LANES, LANES), 0)
    to = lax.broadcasted_iota(jnp.int32, (LANES, LANES), 1)
    shift = chip_ref[0] % per_row * part
    moved = jnp.where(lane == to + shift, jnp.broadcast_to(row, (LANES, LANES)).T, 0.0)
    bias_ref[...] = jnp.sum(moved, axis=0, keepdims=True)[:, :part]


def local(
    features,
    tile_weights,
    tile_rows,
    tile_owners,
    tile_blocks,
    tile_counts,
    cotangent,
    w_self,
    w_neigh,
    bias,
):
    own = features[0].T
    width, node_count = own.shape
    slots, side = tile_weights.shape[1], tile_weights.shape[2]
    batches = lax.axis_size("dp")
    peers = lax.axis_size("x") * LOW
    chips = peers * HIGH
    feats, hidden = w_self.shape
    nodes_here = cotangent.shape[1]
    row_blocks = nodes_here // side
    core = lax.axis_index("core")
    chip = lax.axis_index("x") * HIGH + lax.axis_index("zh")
    chip = chip * LOW + lax.axis_index("zl")
    core_at, chip_at = core[None], chip[None]
    swap = [(i, CORES - 1 - i) for i in range(CORES)]

    copies = call(
        copies_kernel,
        jax.ShapeDtypeStruct((HIGH, width, node_count), BF16),
        [VMEM],
        60,
    )(own)
    whole = lax.all_to_all(copies, "zh", split_axis=0, concat_axis=0, tiled=True)
    half = hidden // CORES
    part = half // chips
    live = jnp.arange(slots, dtype=jnp.int32) < tile_counts[0, 0]
    rows_live = jnp.where(live, tile_rows[0], -1)
    cot, away, weights, half_bias, masked = call(
        functools.partial(split_kernel, part),
        (
            jax.ShapeDtypeStruct((nodes_here, half), BF16),
            jax.ShapeDtypeStruct((nodes_here, half), BF16),
            jax.ShapeDtypeStruct((2 * feats, half), BF16),
            jax.ShapeDtypeStruct((1, half), F32),
            jax.ShapeDtypeStruct((row_blocks * side, slots * side), BF16),
        ),
        [SMEM] + [VMEM] * 4 + [SMEM, VMEM],
        12,
    )(core_at, cotangent[0], w_self, w_neigh, bias[None], rows_live, tile_weights[0])
    their_cot = lax.ppermute(away, "core", swap)
    named = tile_owners[0, :, 0] * row_blocks + tile_blocks[0]
    held = (chip * CORES + core) * row_blocks + jnp.arange(row_blocks, dtype=jnp.int32)
    names = jnp.pad(jnp.concatenate([named, held]), (0, LANES - slots - row_blocks))
    lists = lax.all_gather(names[None], "x", axis=0, tiled=True)
    table = call(
        table_kernel,
        jax.ShapeDtypeStruct((HIGH * width, node_count), BF16),
        [SMEM, VMEM],
        4,
    )(lists, whole)
    other = lax.ppermute(table, "core", swap)
    lists = lax.all_gather(lists, "zl", axis=0, tiled=True)
    columns = CORES * HIGH * width
    sent = call(
        pack_kernel,
        jax.ShapeDtypeStruct((peers, columns, (slots + row_blocks) * side), BF16),
        [SMEM, VMEM, VMEM],
        8,
    )(lists, table, other)
    got = lax.all_to_all(
        sent, ("zl", "x"), split_axis=0, concat_axis=0, tiled=True
    ).reshape(feats, (slots + row_blocks) * side)
    mine = call(
        functools.partial(gather_kernel, width),
        jax.ShapeDtypeStruct((nodes_here, 2 * feats), BF16),
        [SMEM, VMEM, VMEM],
        12,
    )(core_at, got, masked)
    theirs = lax.ppermute(mine, "core", swap)
    rows = 2 * part + SUBLANES
    sums = call(
        layer_kernel,
        jax.ShapeDtypeStruct((chips, rows, feats), BF16),
        [VMEM] * 6,
        16,
    )(mine, theirs, cot, their_cot, weights, half_bias)
    parts = lax.all_to_all(sums, ("x", "zh", "zl"), split_axis=0, concat_axis=0, tiled=True)
    spread = call(
        spread_kernel,
        jax.ShapeDtypeStruct((batches, rows, feats), BF16),
        [VMEM],
        4,
    )(parts)
    totals = lax.all_to_all(spread, "dp", split_axis=0, concat_axis=0, tiled=True)
    out_s, out_n, out_b = call(
        final_kernel,
        (
            jax.ShapeDtypeStruct((part, feats), F32),
            jax.ShapeDtypeStruct((part, feats), F32),
            jax.ShapeDtypeStruct((1, part), F32),
        ),
        [SMEM, VMEM],
        4,
        [pltpu.VMEM((SUBLANES, LANES), F32)],
    )(chip_at, totals)
    return (out_s.T, out_n.T, out_b[0])


def solution(mesh):
    batches = mesh.devices.shape[0]
    split = Mesh(
        mesh.devices.reshape(batches, -1, HIGH, LOW, CORES),
        ("dp", "x", "zh", "zl", "core"),
    )
    feat = ("x", "zh", "zl", "core")
    return jax.shard_map(
        local,
        mesh=split,
        in_specs=(
            P("dp", None, feat),
            P("dp", feat, None, None),
            P("dp", feat),
            P("dp", feat, None),
            P("dp", feat),
            P("dp", feat),
            P("dp", feat, None),
            P(),
            P(),
            P(),
        ),
        out_specs=(P(None, feat), P(None, feat), P(feat)),
        check_vma=False,
    )
```

```python
import functools

import jax
import jax.numpy as jnp
from jax import lax
from jax.experimental import pallas as pl
from jax.experimental.pallas import tpu as pltpu
from jax.sharding import Mesh, PartitionSpec as P

CORES, DEPTH = 2, 8
LANES, SUBLANES = 128, 8
BF16, F32 = jnp.bfloat16, jnp.float32
VMEM = pl.BlockSpec(memory_space=pltpu.VMEM)
SMEM = pl.BlockSpec(memory_space=pltpu.SMEM)
MIB = 1024 * 1024
FIRST = (((0,), (0,)), ((), ()))
LAST = (((1,), (1,)), ((), ()))


def call(kernel, outs, specs, mib, scratch=(), out_spec=VMEM):
    return pl.pallas_call(
        kernel,
        out_shape=outs,
        in_specs=specs,
        out_specs=jax.tree.map(lambda _: out_spec, outs),
        scratch_shapes=list(scratch),
        compiler_params=pltpu.CompilerParams(vmem_limit_bytes=mib * MIB),
    )


def copies_kernel(own_ref, out_ref):
    own = own_ref[...]
    for z in range(out_ref.shape[0]):
        out_ref[z] = own


def pack_kernel(lists_ref, whole_ref, sent_ref, table_ref, chunks_ref, sems):
    depth, width = whole_ref.shape[0], whole_ref.shape[1]
    for z in range(depth):
        table_ref[z * width : (z + 1) * width, :] = whole_ref[z]
    copies = []
    for p in range(chunks_ref.shape[0]):
        for s in range(chunks_ref.shape[2] // LANES):
            at = pl.ds(pl.multiple_of(lists_ref[p, s] * LANES, LANES), LANES)
            chunks_ref[p, :, s * LANES : (s + 1) * LANES] = table_ref[:, at]
        copy = pltpu.make_async_copy(chunks_ref.at[p], sent_ref.at[p], sems.at[p])
        copy.start()
        copies.append(copy)
    for copy in copies:
        copy.wait()


def gather_kernel(width, got_ref, masked_ref, inputs_ref):
    feats = got_ref.shape[0]
    named = masked_ref.shape[1]
    agg = lax.dot_general(
        got_ref[:, :named],
        masked_ref[...],
        LAST,
        preferred_element_type=F32,
    ).astype(BF16)
    row = lax.broadcasted_iota(jnp.int32, (feats, feats), 0)
    feature = lax.broadcasted_iota(jnp.int32, (feats, feats), 1)
    column = row % width
    z = row // width % DEPTH
    reach = feats // (width * DEPTH * CORES)
    x = row // (width * DEPTH) % reach
    core = row // (width * DEPTH * reach)
    place = ((x * DEPTH + z) * CORES + core) * width + column
    order = jnp.where(place == feature, 1.0, 0.0).astype(BF16)
    for k, value in enumerate((got_ref[:, named:], agg)):
        inputs_ref[:, k * feats : (k + 1) * feats] = lax.dot_general(
            value, order, FIRST, preferred_element_type=F32
        ).astype(BF16)


def split_kernel(
    part,
    core_ref,
    cot_ref,
    w_self_ref,
    w_neigh_ref,
    bias_ref,
    rows_ref,
    tiles_ref,
    mine_ref,
    theirs_ref,
    weights_ref,
    half_bias_ref,
    masked_ref,
):
    slots, side = tiles_ref.shape[0], tiles_ref.shape[1]
    for s in range(slots):
        tile = tiles_ref[s]
        for r in range(masked_ref.shape[0] // side):
            masked_ref[r * side : (r + 1) * side, s * side : (s + 1) * side] = jnp.where(
                rows_ref[s] == r, tile, jnp.zeros_like(tile)
            )
    pair = CORES * LANES
    lane = lax.broadcasted_iota(jnp.int32, (pair, LANES), 0)
    to = lax.broadcasted_iota(jnp.int32, (pair, LANES), 1)
    group = to // part * (CORES * part) + to % part
    here = jnp.where(lane == group + core_ref[0] * part, 1.0, 0.0)
    there = jnp.where(lane == group + (1 - core_ref[0]) * part, 1.0, 0.0)
    here16, there16 = here.astype(BF16), there.astype(BF16)
    feats = w_self_ref.shape[0]

    def pick(value, chosen):
        return jnp.dot(value, chosen, preferred_element_type=F32).astype(BF16)

    for m in range(mine_ref.shape[1] // LANES):
        out = slice(m * LANES, (m + 1) * LANES)
        wide = slice(m * pair, (m + 1) * pair)
        mine_ref[:, out] = pick(cot_ref[:, wide], here16)
        theirs_ref[:, out] = pick(cot_ref[:, wide], there16)
        weights_ref[:feats, out] = pick(w_self_ref[:, wide], here16)
        weights_ref[feats:, out] = pick(w_neigh_ref[:, wide], here16)
        half_bias_ref[:, out] = jnp.dot(
            jnp.broadcast_to(bias_ref[:, wide], (SUBLANES, pair)),
            here,
            precision=lax.Precision.HIGHEST,
            preferred_element_type=F32,
        )[:1]


def layer_kernel(
    mine_ref, theirs_ref, cot_ref, their_cot_ref, weights_ref, bias_ref, sent_ref
):
    half = cot_ref.shape[1]
    weights, bias = weights_ref[...], bias_ref[...]
    total, sums = 0.0, 0.0
    for inputs, cot in (
        (mine_ref[...], cot_ref[...]),
        (theirs_ref[...], their_cot_ref[...]),
    ):
        pre = jnp.dot(inputs, weights, preferred_element_type=F32) + bias
        s = jax.nn.sigmoid(pre)
        slope = (cot.astype(F32) * (s * (1.0 + pre * (1.0 - s)))).astype(BF16)
        total += lax.dot_general(slope, inputs, FIRST, preferred_element_type=F32)
        sums += jnp.sum(slope.astype(F32), axis=0, keepdims=True)
    chips, rows = sent_ref.shape[0], sent_ref.shape[1]
    part = half // chips
    feats = total.shape[1] // 2
    total = total.astype(BF16)
    tail = jnp.concatenate(
        [sums[:, k * LANES : (k + 1) * LANES] for k in range(half // LANES)]
        + [jnp.zeros((SUBLANES - half // LANES, LANES), F32)],
        axis=0,
    ).astype(BF16)
    for k in range(chips):
        here = slice(k * part, (k + 1) * part)
        sent_ref[k, :part, :] = total[here, :feats]
        sent_ref[k, part : 2 * part, :] = total[here, feats:]
        sent_ref[k, 2 * part : rows, :] = tail


def spread_kernel(got_ref, out_ref):
    total = jnp.sum(got_ref[...].astype(F32), axis=0).astype(BF16)
    for b in range(out_ref.shape[0]):
        out_ref[b] = total


def final_kernel(chip_ref, got_ref, self_ref, neigh_ref, bias_ref, sums_ref):
    part = self_ref.shape[0]
    total = jnp.sum(got_ref[...].astype(F32), axis=0)
    self_ref[...] = total[:part]
    neigh_ref[...] = total[part : 2 * part]
    sums_ref[...] = total[2 * part :]
    per_row = LANES // part
    row = sums_ref[pl.ds(chip_ref[0] // per_row, 1), :]
    lane = lax.broadcasted_iota(jnp.int32, (LANES, LANES), 0)
    to = lax.broadcasted_iota(jnp.int32, (LANES, LANES), 1)
    shift = chip_ref[0] % per_row * part
    moved = jnp.where(lane == to + shift, jnp.broadcast_to(row, (LANES, LANES)).T, 0.0)
    bias_ref[...] = jnp.sum(moved, axis=0, keepdims=True)[:, :part]


def local(
    features,
    tile_weights,
    tile_rows,
    tile_owners,
    tile_blocks,
    tile_counts,
    cotangent,
    w_self,
    w_neigh,
    bias,
):
    own = features[0].T
    width, node_count = own.shape
    slots, side = tile_weights.shape[1], tile_weights.shape[2]
    batches = lax.axis_size("dp")
    peers = lax.axis_size("x") * CORES
    chips = lax.axis_size("x") * DEPTH
    feats, hidden = w_self.shape
    nodes_here = cotangent.shape[1]
    row_blocks = nodes_here // side
    core = lax.axis_index("core")
    chip = lax.axis_index("x") * DEPTH + lax.axis_index("z")
    core_at, chip_at = core[None], chip[None]
    swap = [(i, CORES - 1 - i) for i in range(CORES)]

    copies = call(
        copies_kernel,
        jax.ShapeDtypeStruct((DEPTH, width, node_count), BF16),
        [VMEM],
        60,
    )(own)
    whole = lax.all_to_all(copies, "z", split_axis=0, concat_axis=0, tiled=True)
    half = hidden // CORES
    part = half // chips
    live = jnp.arange(slots, dtype=jnp.int32) < tile_counts[0, 0]
    rows_live = jnp.where(live, tile_rows[0], -1)
    cot, away, weights, half_bias, masked = call(
        functools.partial(split_kernel, part),
        (
            jax.ShapeDtypeStruct((nodes_here, half), BF16),
            jax.ShapeDtypeStruct((nodes_here, half), BF16),
            jax.ShapeDtypeStruct((2 * feats, half), BF16),
            jax.ShapeDtypeStruct((1, half), F32),
            jax.ShapeDtypeStruct((row_blocks * side, slots * side), BF16),
        ),
        [SMEM] + [VMEM] * 4 + [SMEM, VMEM],
        12,
    )(core_at, cotangent[0], w_self, w_neigh, bias[None], rows_live, tile_weights[0])
    their_cot = lax.ppermute(away, "core", swap)
    named = tile_owners[0, :, 0] * row_blocks + tile_blocks[0]
    held = (chip * CORES + core) * row_blocks + jnp.arange(row_blocks, dtype=jnp.int32)
    names = jnp.pad(jnp.concatenate([named, held]), (0, LANES - slots - row_blocks))
    lists = lax.all_gather(names[None], ("core", "x"), axis=0, tiled=True)
    columns = DEPTH * width
    chunks = (peers, columns, (slots + row_blocks) * side)
    sent = call(
        pack_kernel,
        jax.ShapeDtypeStruct(chunks, BF16),
        [SMEM, VMEM],
        8,
        [
            pltpu.VMEM((columns, node_count), BF16),
            pltpu.VMEM(chunks, BF16),
            pltpu.SemaphoreType.DMA((peers,)),
        ],
        pl.BlockSpec(memory_space=pl.ANY),
    )(lists, whole)
    got = lax.all_to_all(
        sent, ("core", "x"), split_axis=0, concat_axis=0, tiled=True
    ).reshape(feats, (slots + row_blocks) * side)
    mine = call(
        functools.partial(gather_kernel, width),
        jax.ShapeDtypeStruct((nodes_here, 2 * feats), BF16),
        [VMEM, VMEM],
        12,
    )(got, masked)
    theirs = lax.ppermute(mine, "core", swap)
    rows = 2 * part + SUBLANES
    sums = call(
        layer_kernel,
        jax.ShapeDtypeStruct((chips, rows, feats), BF16),
        [VMEM] * 6,
        16,
    )(mine, theirs, cot, their_cot, weights, half_bias)
    parts = lax.all_to_all(sums, ("x", "z"), split_axis=0, concat_axis=0, tiled=True)
    spread = call(
        spread_kernel,
        jax.ShapeDtypeStruct((batches, rows, feats), BF16),
        [VMEM],
        4,
    )(parts)
    totals = lax.all_to_all(spread, "dp", split_axis=0, concat_axis=0, tiled=True)
    out_s, out_n, out_b = call(
        final_kernel,
        (
            jax.ShapeDtypeStruct((part, feats), F32),
            jax.ShapeDtypeStruct((part, feats), F32),
            jax.ShapeDtypeStruct((1, part), F32),
        ),
        [SMEM, VMEM],
        4,
        [pltpu.VMEM((SUBLANES, LANES), F32)],
    )(chip_at, totals)
    return (out_s.T, out_n.T, out_b[0])


def solution(mesh):
    batches, owners = mesh.devices.shape
    split = Mesh(
        mesh.devices.reshape(batches, owners // (DEPTH * CORES), DEPTH, CORES),
        ("dp", "x", "z", "core"),
    )
    feat = ("x", "z", "core")
    return jax.shard_map(
        local,
        mesh=split,
        in_specs=(
            P("dp", None, feat),
            P("dp", feat, None, None),
            P("dp", feat),
            P("dp", feat, None),
            P("dp", feat),
            P("dp", feat),
            P("dp", feat, None),
            P(),
            P(),
            P(),
        ),
        out_specs=(P(None, feat), P(None, feat), P(feat)),
        check_vma=False,
    )
```

```python
import functools

import jax
import jax.numpy as jnp
from jax import lax
from jax.experimental import pallas as pl
from jax.experimental.pallas import tpu as pltpu
from jax.sharding import Mesh, PartitionSpec as P

CORES, DEPTH = 2, 8
LANES, SUBLANES = 128, 8
BF16, F32 = jnp.bfloat16, jnp.float32
VMEM = pl.BlockSpec(memory_space=pltpu.VMEM)
SMEM = pl.BlockSpec(memory_space=pltpu.SMEM)
MIB = 1024 * 1024
FIRST = (((0,), (0,)), ((), ()))
LAST = (((1,), (1,)), ((), ()))


def call(kernel, outs, specs, mib, scratch=(), out_spec=VMEM):
    return pl.pallas_call(
        kernel,
        out_shape=outs,
        in_specs=specs,
        out_specs=jax.tree.map(lambda _: out_spec, outs),
        scratch_shapes=list(scratch),
        compiler_params=pltpu.CompilerParams(vmem_limit_bytes=mib * MIB),
    )


def copies_kernel(own_ref, out_ref):
    own = own_ref[...]
    for z in range(out_ref.shape[0]):
        out_ref[z] = own


def pack_kernel(lists_ref, whole_ref, sent_ref, table_ref, chunks_ref, sems):
    table_ref[...] = whole_ref[...].reshape(table_ref.shape)
    reach = chunks_ref.shape[0] // CORES
    copies = []
    for p in range(chunks_ref.shape[0]):
        device = p % reach * CORES + p // reach
        for s in range(chunks_ref.shape[2] // LANES):
            at = pl.ds(pl.multiple_of(lists_ref[device, s] * LANES, LANES), LANES)
            chunks_ref[p, :, s * LANES : (s + 1) * LANES] = table_ref[:, at]
        copy = pltpu.make_async_copy(chunks_ref.at[p], sent_ref.at[p], sems.at[p])
        copy.start()
        copies.append(copy)
    for copy in copies:
        copy.wait()


def gather_kernel(width, got_ref, masked_ref, inputs_ref):
    feats = got_ref.shape[0]
    named = masked_ref.shape[1]
    agg = lax.dot_general(
        got_ref[:, :named],
        masked_ref[...],
        LAST,
        preferred_element_type=F32,
    ).astype(BF16)
    row = lax.broadcasted_iota(jnp.int32, (feats, feats), 0)
    feature = lax.broadcasted_iota(jnp.int32, (feats, feats), 1)
    column = row % width
    z = row // width % DEPTH
    reach = feats // (width * DEPTH * CORES)
    x = row // (width * DEPTH) % reach
    core = row // (width * DEPTH * reach)
    place = ((x * DEPTH + z) * CORES + core) * width + column
    order = jnp.where(place == feature, 1.0, 0.0).astype(BF16)
    for k, value in enumerate((got_ref[:, named:], agg)):
        inputs_ref[:, k * feats : (k + 1) * feats] = lax.dot_general(
            value, order, FIRST, preferred_element_type=F32
        ).astype(BF16)


def split_kernel(
    part,
    core_ref,
    cot_ref,
    w_self_ref,
    w_neigh_ref,
    bias_ref,
    rows_ref,
    tiles_ref,
    mine_ref,
    theirs_ref,
    weights_ref,
    half_bias_ref,
    masked_ref,
):
    slots, side = tiles_ref.shape[0], tiles_ref.shape[1]
    for s in range(slots):
        tile = tiles_ref[s]
        for r in range(masked_ref.shape[0] // side):
            masked_ref[r * side : (r + 1) * side, s * side : (s + 1) * side] = jnp.where(
                rows_ref[s] == r, tile, jnp.zeros_like(tile)
            )
    pair = CORES * LANES
    lane = lax.broadcasted_iota(jnp.int32, (pair, LANES), 0)
    to = lax.broadcasted_iota(jnp.int32, (pair, LANES), 1)
    group = to // part * (CORES * part) + to % part
    here = jnp.where(lane == group + core_ref[0] * part, 1.0, 0.0)
    there = jnp.where(lane == group + (1 - core_ref[0]) * part, 1.0, 0.0)
    here16, there16 = here.astype(BF16), there.astype(BF16)
    feats = w_self_ref.shape[0]

    def pick(value, chosen):
        return jnp.dot(value, chosen, preferred_element_type=F32).astype(BF16)

    for m in range(mine_ref.shape[1] // LANES):
        out = slice(m * LANES, (m + 1) * LANES)
        wide = slice(m * pair, (m + 1) * pair)
        mine_ref[:, out] = pick(cot_ref[:, wide], here16)
        theirs_ref[:, out] = pick(cot_ref[:, wide], there16)
        weights_ref[:feats, out] = pick(w_self_ref[:, wide], here16)
        weights_ref[feats:, out] = pick(w_neigh_ref[:, wide], here16)
        half_bias_ref[:, out] = jnp.dot(
            jnp.broadcast_to(bias_ref[:, wide], (SUBLANES, pair)),
            here,
            precision=lax.Precision.HIGHEST,
            preferred_element_type=F32,
        )[:1]


def layer_kernel(
    mine_ref, theirs_ref, cot_ref, their_cot_ref, weights_ref, bias_ref, sent_ref
):
    half = cot_ref.shape[1]
    weights, bias = weights_ref[...], bias_ref[...]
    total, sums = 0.0, 0.0
    for inputs, cot in (
        (mine_ref[...], cot_ref[...]),
        (theirs_ref[...], their_cot_ref[...]),
    ):
        pre = jnp.dot(inputs, weights, preferred_element_type=F32) + bias
        s = jax.nn.sigmoid(pre)
        slope = (cot.astype(F32) * (s * (1.0 + pre * (1.0 - s)))).astype(BF16)
        total += lax.dot_general(slope, inputs, FIRST, preferred_element_type=F32)
        sums += jnp.sum(slope.astype(F32), axis=0, keepdims=True)
    chips, rows = sent_ref.shape[0], sent_ref.shape[1]
    part = half // chips
    feats = total.shape[1] // 2
    total = total.astype(BF16)
    tail = jnp.concatenate(
        [sums[:, k * LANES : (k + 1) * LANES] for k in range(half // LANES)]
        + [jnp.zeros((SUBLANES - half // LANES, LANES), F32)],
        axis=0,
    ).astype(BF16)
    for k in range(chips):
        here = slice(k * part, (k + 1) * part)
        sent_ref[k, :part, :] = total[here, :feats]
        sent_ref[k, part : 2 * part, :] = total[here, feats:]
        sent_ref[k, 2 * part : rows, :] = tail


def spread_kernel(got_ref, out_ref):
    total = jnp.sum(got_ref[...].astype(F32), axis=0).astype(BF16)
    for b in range(out_ref.shape[0]):
        out_ref[b] = total


def final_kernel(chip_ref, got_ref, self_ref, neigh_ref, bias_ref, sums_ref):
    part = self_ref.shape[0]
    total = jnp.sum(got_ref[...].astype(F32), axis=0)
    self_ref[...] = total[:part]
    neigh_ref[...] = total[part : 2 * part]
    sums_ref[...] = total[2 * part :]
    per_row = LANES // part
    row = sums_ref[pl.ds(chip_ref[0] // per_row, 1), :]
    lane = lax.broadcasted_iota(jnp.int32, (LANES, LANES), 0)
    to = lax.broadcasted_iota(jnp.int32, (LANES, LANES), 1)
    shift = chip_ref[0] % per_row * part
    moved = jnp.where(lane == to + shift, jnp.broadcast_to(row, (LANES, LANES)).T, 0.0)
    bias_ref[...] = jnp.sum(moved, axis=0, keepdims=True)[:, :part]


def local(
    features,
    tile_weights,
    tile_rows,
    tile_owners,
    tile_blocks,
    tile_counts,
    cotangent,
    w_self,
    w_neigh,
    bias,
):
    own = features[0].T
    width, node_count = own.shape
    slots, side = tile_weights.shape[1], tile_weights.shape[2]
    batches = lax.axis_size("dp")
    peers = lax.axis_size("x") * CORES
    chips = lax.axis_size("x") * DEPTH
    feats, hidden = w_self.shape
    nodes_here = cotangent.shape[1]
    row_blocks = nodes_here // side
    core = lax.axis_index("core")
    chip = lax.axis_index("x") * DEPTH + lax.axis_index("z")
    core_at, chip_at = core[None], chip[None]
    swap = [(i, CORES - 1 - i) for i in range(CORES)]

    copies = call(
        copies_kernel,
        jax.ShapeDtypeStruct((DEPTH, width, node_count), BF16),
        [VMEM],
        60,
    )(own)
    whole = lax.all_to_all(copies, "z", split_axis=0, concat_axis=0, tiled=True)
    half = hidden // CORES
    part = half // chips
    live = jnp.arange(slots, dtype=jnp.int32) < tile_counts[0, 0]
    rows_live = jnp.where(live, tile_rows[0], -1)
    cot, away, weights, half_bias, masked = call(
        functools.partial(split_kernel, part),
        (
            jax.ShapeDtypeStruct((nodes_here, half), BF16),
            jax.ShapeDtypeStruct((nodes_here, half), BF16),
            jax.ShapeDtypeStruct((2 * feats, half), BF16),
            jax.ShapeDtypeStruct((1, half), F32),
            jax.ShapeDtypeStruct((row_blocks * side, slots * side), BF16),
        ),
        [SMEM] + [VMEM] * 4 + [SMEM, VMEM],
        12,
    )(core_at, cotangent[0], w_self, w_neigh, bias[None], rows_live, tile_weights[0])
    their_cot = lax.ppermute(away, "core", swap)
    named = tile_owners[0, :, 0] * row_blocks + tile_blocks[0]
    held = (chip * CORES + core) * row_blocks + jnp.arange(row_blocks, dtype=jnp.int32)
    names = jnp.pad(jnp.concatenate([named, held]), (0, LANES - slots - row_blocks))
    lists = lax.all_gather(names[None], ("x", "core"), axis=0, tiled=True)
    columns = DEPTH * width
    chunks = (peers, columns, (slots + row_blocks) * side)
    sent = call(
        pack_kernel,
        jax.ShapeDtypeStruct(chunks, BF16),
        [SMEM, VMEM],
        8,
        [
            pltpu.VMEM((columns, node_count), BF16),
            pltpu.VMEM(chunks, BF16),
            pltpu.SemaphoreType.DMA((peers,)),
        ],
        pl.BlockSpec(memory_space=pl.ANY),
    )(lists, whole)
    got = lax.all_to_all(
        sent, ("core", "x"), split_axis=0, concat_axis=0, tiled=True
    ).reshape(feats, (slots + row_blocks) * side)
    mine = call(
        functools.partial(gather_kernel, width),
        jax.ShapeDtypeStruct((nodes_here, 2 * feats), BF16),
        [VMEM, VMEM],
        12,
    )(got, masked)
    theirs = lax.ppermute(mine, "core", swap)
    rows = 2 * part + SUBLANES
    sums = call(
        layer_kernel,
        jax.ShapeDtypeStruct((chips, rows, feats), BF16),
        [VMEM] * 6,
        16,
    )(mine, theirs, cot, their_cot, weights, half_bias)
    parts = lax.all_to_all(sums, ("x", "z"), split_axis=0, concat_axis=0, tiled=True)
    spread = call(
        spread_kernel,
        jax.ShapeDtypeStruct((batches, rows, feats), BF16),
        [VMEM],
        4,
    )(parts)
    totals = lax.all_to_all(spread, "dp", split_axis=0, concat_axis=0, tiled=True)
    out_s, out_n, out_b = call(
        final_kernel,
        (
            jax.ShapeDtypeStruct((part, feats), F32),
            jax.ShapeDtypeStruct((part, feats), F32),
            jax.ShapeDtypeStruct((1, part), F32),
        ),
        [SMEM, VMEM],
        4,
        [pltpu.VMEM((SUBLANES, LANES), F32)],
    )(chip_at, totals)
    return (out_s.T, out_n.T, out_b[0])


def solution(mesh):
    batches, owners = mesh.devices.shape
    split = Mesh(
        mesh.devices.reshape(batches, owners // (DEPTH * CORES), DEPTH, CORES),
        ("dp", "x", "z", "core"),
    )
    feat = ("x", "z", "core")
    return jax.shard_map(
        local,
        mesh=split,
        in_specs=(
            P("dp", None, feat),
            P("dp", feat, None, None),
            P("dp", feat),
            P("dp", feat, None),
            P("dp", feat),
            P("dp", feat),
            P("dp", feat, None),
            P(),
            P(),
            P(),
        ),
        out_specs=(P(None, feat), P(None, feat), P(feat)),
        check_vma=False,
    )
```
